128 devices in a mesh: section: 8 (over y, x_lo), fsdp: 16 (over z, x_hi, core).
Axes of the slice: x: 4 (x_hi: 2, x_lo: 2; x = x_hi * 2 + x_lo), y: 4, z: 4, core: 2. Of those that a mesh axis runs over, the one named last changes fastest.
Arguments:
- inputs: bfloat16 [8, 2, 2048, 8192], P('section', None, 'fsdp'), may hold values from -6 to 6
- queries: bfloat16 [8, 2, 2048, 8192], P('section', None, 'fsdp'), may hold values from -14 to 14, as said below
- top_cotangent: bfloat16 [2, 2048, 8192], P(None, 'fsdp'), may hold values from -6 to 6
- key_weight: bfloat16 [8, 8192, 512], P('section', 'fsdp'), may hold values from -0.0625 to 0.0625
- value_weight: bfloat16 [8, 8192, 512], P('section', 'fsdp'), may hold values from -0.0625 to 0.0625
- order: int32 [2], replicated, may hold values from 0 to 1, each once
- doc_lengths: int32 [2, 16, 4], P(None, 'fsdp'), may hold values from 1 to 64, 128 in all within a row
Outputs:
- grads: bfloat16 [8, 2, 2048, 8192], P('section', None, 'fsdp')
The draws below stay inside these ranges and needn't reach their ends.
Inputs may be any that keep to these rules, and one draw needn't show every extreme that they name: `queries`: query entries are of order one, or rows scaled by up to 8. `doc_lengths`: each row sums to 128; the largest length is 64.
All inputs are finite; a program needn't handle non-finite values.
Results may differ from the reference program's by a relative error of at most 0.035.
Values may be sent and summed in bfloat16 or wider, within the bound.
A program may use at most 128 MiB of HBM per device.

```python
import math
import jax
import jax.numpy as jnp
import numpy as np
from jax import lax

HEADS = 64
KV_HEADS = 4
HEAD_DIM = 128
D = 8192
MB = 2
TOK_DEV = 128
DOCS = 4
KVW = 512
SECTIONS = 8
TOKENS = 2048
N_SECTION = 8
N_FSDP = 16


def draw_queries(key, part):
    key = jax.random.fold_in(key, 7)
    shape = (SECTIONS, MB, TOKENS, D)
    return jnp.clip(jax.random.normal(key, shape, jnp.float32), -5.0, 5.0).astype(jnp.bfloat16)


def block_levels(stream_key, extent, shards, low, largest):
    def one(axis_at, shards_of):
        steps = jax.random.uniform(jax.random.fold_in(jax.random.fold_in(stream_key, 6), axis_at), (shards_of,), jnp.float32, low / len(shards), largest / len(shards))
        return jnp.repeat(jnp.exp(steps), extent[axis_at] // shards_of).reshape((-1,) + (1,) * (len(extent) - axis_at - 1))

    loudness = one(*shards[0])
    for cut in shards[1:]:
        loudness = loudness * one(*cut)
    return loudness


def length_profile(count, total, reach, skew):
    weights = [(1 << 20) // math.isqrt(standing ** skew) + 1 for standing in range(2, count + 1)]
    spare, counts = total - reach - (count - 1), [1] * (count - 1)
    while spare > 0:
        movable = [i for i in range(count - 1) if counts[i] < reach]
        whole, left = sum([weights[i] for i in movable]), spare
        for i in movable:
            more = min(reach - counts[i], max(1, left * weights[i] // whole), spare)
            counts[i] = counts[i] + more
            spare = spare - more
    return np.array([reach] + counts)


def uneven_parts(rng, count, total, bound, slope):
    if count == 2:
        one = jax.random.randint(rng, (), max(1, total - bound), min(bound, total - 1) + 1)
        return jnp.stack([one, total - one])
    tallies = jnp.asarray(length_profile(count, total, bound, slope), jnp.int32)
    couples = (count - 1) // 2
    donor, taker = tallies[1:1 + 2 * couples:2], tallies[2:2 + 2 * couples:2]
    slack = jnp.minimum(donor - 1, bound - taker)
    passed = jax.random.randint(jax.random.fold_in(rng, 1), (couples,), 0, 1 << 20) % (slack + 1)
    tallies = tallies.at[1:1 + 2 * couples:2].set(donor - passed).at[2:2 + 2 * couples:2].set(taker + passed)
    return tallies[jax.random.permutation(jax.random.fold_in(rng, 2), count)]


def centred(stream_key, extent, deviation, most, split=(), kind=jnp.bfloat16):
    result = deviation * jax.random.normal(stream_key, extent, jnp.float32)
    if split:
        result = result * block_levels(stream_key, extent, split, -0.22, 0.18)
    return jnp.clip(result, -most, most).astype(kind)


def setup_inputs(seed: int = 0) -> dict:
    splits = jax.random.split(jax.random.key(seed), 8)
    return {
        "inputs": centred(splits[0], (SECTIONS, MB, TOKENS, D), 1.0, 6.0, ((0, 8), (2, 16))),
        "queries": draw_queries(jax.random.fold_in(splits[7], 71), 0),
        "top_cotangent": centred(splits[2], (MB, TOKENS, D), 1.0, 6.0, ((1, 16),)),
        "key_weight": centred(splits[3], (SECTIONS, D, KVW), D ** -0.5, 0.0625, ((0, 8), (1, 16))),
        "value_weight": centred(splits[4], (SECTIONS, D, KVW), D ** -0.5, 0.0625, ((0, 8), (1, 16))),
        "order": jax.random.permutation(splits[5], MB).astype(jnp.int32),
        "doc_lengths": jax.vmap(lambda own: uneven_parts(own, DOCS, TOK_DEV, TOK_DEV // 2, 2))(jax.random.split(splits[6], MB * N_FSDP)).reshape((MB, N_FSDP, DOCS)).astype(jnp.int32),
    }


def segment_ids(lengths, rows):
    ends = jnp.cumsum(lengths)
    pos = jnp.arange(rows, dtype=jnp.int32)
    return lax.optimization_barrier(jnp.sum((pos[:, None] >= ends[None, :]).astype(jnp.int32), axis=1))

def block_grad(queries_blk, keys_blk, values_blk, up_blk, seg):
    rows = queries_blk.shape[0]
    group = HEADS // KV_HEADS
    scale = 1.0 / HEAD_DIM ** 0.5
    qh = queries_blk.reshape(rows, KV_HEADS, group, HEAD_DIM).astype(jnp.float32)
    kh = keys_blk.reshape(rows, KV_HEADS, HEAD_DIM).astype(jnp.float32)
    vh = values_blk.reshape(rows, KV_HEADS, HEAD_DIM).astype(jnp.float32)
    uh = up_blk.reshape(rows, KV_HEADS, group, HEAD_DIM).astype(jnp.float32)
    pos = jnp.arange(rows, dtype=jnp.int32)
    allowed = (seg[:, None] == seg[None, :]) & (pos[None, :] <= pos[:, None])
    scores = jnp.einsum('ikgd,jkd->kgij', qh, kh) * scale
    scores = jnp.where(allowed, scores, jnp.float32(-1e+30))
    top = lax.optimization_barrier(jnp.max(scores, axis=-1, keepdims=True))
    weights = jnp.exp(scores - top)
    probs = weights / lax.optimization_barrier(jnp.sum(weights, axis=-1, keepdims=True))
    dprobs = jnp.einsum('ikgd,jkd->kgij', uh, vh)
    delta = lax.optimization_barrier(jnp.sum(probs * dprobs, axis=-1, keepdims=True))
    dscores = (probs * (dprobs - delta) * scale).astype(jnp.bfloat16)
    probs_rounded = probs.astype(jnp.bfloat16)
    dvalues = jnp.einsum('kgij,ikgd->jkd', probs_rounded.astype(jnp.float32), uh)
    dkeys = jnp.einsum('kgij,ikgd->jkd', dscores.astype(jnp.float32), qh)
    width = KV_HEADS * HEAD_DIM
    return (dkeys.reshape(rows, width).astype(jnp.bfloat16), dvalues.reshape(rows, width).astype(jnp.bfloat16))

def reference(inputs, queries, top_cotangent, key_weight, value_weight, order, doc_lengths):
    blocks = N_FSDP
    width = KV_HEADS * HEAD_DIM
    cotangent = top_cotangent
    per_layer = []
    for layer in range(N_SECTION - 1, -1, -1):
        both = jnp.concatenate([key_weight[layer], value_weight[layer]], axis=1)
        fresh = []
        for micro in range(MB):
            acts = inputs[layer, micro]
            keyval = jnp.dot(acts, both, preferred_element_type=jnp.float32).astype(jnp.bfloat16)
            up = cotangent[micro]

            def one_block(pieces):
                q_blk, kv_blk, up_blk, lens = pieces
                seg = segment_ids(lens, TOK_DEV)
                dk, dv = block_grad(q_blk, kv_blk[:, :width], kv_blk[:, width:], up_blk, seg)
                return jnp.concatenate([dk, dv], axis=1)
            dkv = lax.map(one_block, (queries[layer, micro].reshape(blocks, TOK_DEV, D), keyval.reshape(blocks, TOK_DEV, 2 * width), up.reshape(blocks, TOK_DEV, D), doc_lengths[micro]))
            dkv = dkv.reshape(blocks * TOK_DEV, 2 * width)
            back = lax.dot_general(dkv, both, (((1,), (1,)), ((), ())), preferred_element_type=jnp.float32)
            fresh.append((up.astype(jnp.float32) + back).astype(jnp.bfloat16))
        cotangent = jnp.stack(fresh)
        per_layer.append(cotangent)
    grads = jnp.stack(per_layer[::-1])
    return grads[:, order]
```

```python
import functools
import math

import jax
import jax.numpy as jnp
from jax import lax
from jax.experimental import pallas as pl
from jax.experimental.pallas import tpu as pltpu
from jax.sharding import PartitionSpec as P

MESH = pl.DeviceIdType.MESH
HEADS = 64
KV_HEADS = 4
GROUP = HEADS // KV_HEADS
HEAD_DIM = 128
ROWS = 16
LONGEST = 64
WINDOW = LONGEST + ROWS
NT = (((1,), (1,)), ((), ()))


def kernel(
    sections, micros, tokens,
    acts_hbm, q_hbm, top_hbm, kw_hbm, vw_hbm, lens, out_hbm,
    wt, acts, q, up, down, raw, kv_acc, kv, pt, acc,
    load_sem, out_sem, gather_send, gather_recv, chain_send, chain_recv,
):
    section, f = lax.axis_index("section"), lax.axis_index("fsdp")
    z, h, c = f // 4, (f // 2) % 2, f % 2
    shard = raw.shape[1]
    width = raw.shape[2]
    piece = GROUP * HEAD_DIM
    per_micro = tokens // ROWS
    chunks = micros * per_micro

    def index(dz, dh, dc):
        return 4 * ((z + dz + 4) % 4) + 2 * ((h + dh) % 2) + (c + dc) % 2

    z_next, z_prev = (section, index(1, 0, 0)), (section, index(-1, 0, 0))
    x_pair, core_pair = (section, index(0, 1, 0)), (section, index(0, 0, 1))
    onward = ((section + sections - 1) % sections, f)
    before = ((section + 1) % sections, f)

    loads = [
        pltpu.make_async_copy(kw_hbm, raw.at[0], load_sem.at[0]),
        pltpu.make_async_copy(vw_hbm, raw.at[1], load_sem.at[1]),
        pltpu.make_async_copy(acts_hbm, acts, load_sem.at[2]),
        pltpu.make_async_copy(q_hbm, q, load_sem.at[3]),
    ]
    for load in loads:
        load.start()
    load_top = pltpu.make_async_copy(top_hbm, up, load_sem.at[4])

    @pl.when(section == sections - 1)
    def _():
        load_top.start()

    barrier = pltpu.get_barrier_semaphore()
    for device in (z_next, z_prev, x_pair, core_pair, onward, before):
        pl.semaphore_signal(barrier, inc=1, device_id=device, device_id_type=MESH)

    for part in range(2):
        loads[part].wait()
        wt[f, part * width:(part + 1) * width, :] = jnp.transpose(raw[part])
    pl.semaphore_wait(barrier, 6)

    def copy(role, half, owner, device):
        block = wt.at[owner, pl.ds(half * width, width), :]
        return pltpu.make_async_remote_copy(
            src_ref=block, dst_ref=block,
            send_sem=gather_send.at[role, half], recv_sem=gather_recv.at[role, half],
            device_id=device, device_id_type=MESH,
        )

    sent = []

    def send(role, half, owner, device):
        copy(role, half, owner, device).start()
        sent.append((role, half, owner, device))

    def arrive(role, half, owner, device):
        copy(role, half, owner, device).wait_recv()

    places = [(0, 0), (-1, 0), (1, 0), (0, 1), (2, 0), (-1, 1), (1, 1), (2, 1)]
    own = index(0, 0, 0)

    def to_core(place, half):
        send(7 + place, half, index(*places[place], 0), core_pair)

    def from_core(place):
        for half in range(2):
            arrive(7 + place, half, index(*places[place], 1), core_pair)

    def add_keyval(dz, dh):
        def one(dc, carry):
            owner = index(dz, dh, dc)
            cols = pl.ds(pl.multiple_of(owner * shard, shard), shard)
            kv_acc[...] += lax.dot_general(
                acts[:, cols], wt[owner], NT, preferred_element_type=jnp.float32
            )
            return carry

        lax.fori_loop(0, 2, one, 0)

    for half in range(2):
        send(0, half, own, z_next)
        send(1, half, own, z_prev)
        send(2, half, own, x_pair)
    for half in range(2):
        to_core(0, half)
    kv_acc[...] = jnp.zeros_like(kv_acc)
    acc[...] = jnp.zeros_like(acc)
    loads[2].wait()
    loads[3].wait()
    from_core(0)
    add_keyval(0, 0)

    for half in range(2):
        arrive(0, half, index(-1, 0, 0), z_prev)
        if half == 0:
            send(3, half, index(-1, 0, 0), z_next)
        to_core(1, half)
        arrive(1, half, index(1, 0, 0), z_next)
        if half == 1:
            send(3, half, index(1, 0, 0), z_prev)
        to_core(2, half)
        arrive(2, half, index(0, 1, 0), x_pair)
        send(4, half, index(0, 1, 0), z_next)
        send(5, half, index(0, 1, 0), z_prev)
        to_core(3, half)
    for place in (1, 2, 3):
        from_core(place)
        add_keyval(*places[place])
    for half in range(2):
        arrive(3, half, index(2, 0, 0), z_prev if half == 0 else z_next)
        send(6, half, index(2, 0, 0), x_pair)
        to_core(4, half)
        if half == 1:
            from_core(4)
            add_keyval(*places[4])
        arrive(4, half, index(-1, 1, 0), z_prev)
        to_core(5, half)
        arrive(5, half, index(1, 1, 0), z_next)
        to_core(6, half)
    for place in (5, 6):
        from_core(place)
        add_keyval(*places[place])
    for half in range(2):
        arrive(6, half, index(2, 1, 0), x_pair)
        to_core(7, half)
    from_core(7)
    add_keyval(*places[7])
    kv[...] = kv_acc[...].astype(jnp.bfloat16)

    def place_of(chunk):
        micro = chunk // per_micro
        first = tokens - ROWS - ROWS * (chunk % per_micro)
        base = micro * tokens
        row = pl.multiple_of(base + first, ROWS)
        low = jnp.maximum(first - LONGEST, 0)
        return micro, first, row, low, pl.multiple_of(base + low, ROWS)

    def stacked(ref, row, k):
        return jnp.concatenate(
            [
                ref[pl.ds(row, ROWS), (GROUP * k + g) * HEAD_DIM:(GROUP * k + g + 1) * HEAD_DIM]
                for g in range(GROUP)
            ],
            axis=0,
        )

    def scores(chunk):
        micro, first, row, low, low_row = place_of(chunk)
        end0 = lens[micro, 0]
        end1 = end0 + lens[micro, 1]
        end2 = end1 + lens[micro, 2]
        shape = (WINDOW, GROUP * ROWS)
        i = first + lax.broadcasted_iota(jnp.int32, (1, shape[1]), 1) % ROWS
        begin = jnp.where(i >= end2, end2, jnp.where(i >= end1, end1, jnp.where(i >= end0, end0, 0)))
        j = low + lax.broadcasted_iota(jnp.int32, shape, 0)
        allowed = (j >= begin) & (j <= i)
        for k in range(KV_HEADS):
            keys = kv[pl.ds(low_row, WINDOW), k * HEAD_DIM:(k + 1) * HEAD_DIM]
            s = lax.dot_general(keys, stacked(q, row, k), NT, preferred_element_type=jnp.float32)
            s = jnp.where(allowed, s * (math.log2(math.e) / HEAD_DIM**0.5), -1e30)
            weights = jnp.exp2(s - jnp.max(s, axis=0, keepdims=True))
            probs = weights / jnp.sum(weights, axis=0, keepdims=True)
            pt[k] = probs.astype(jnp.bfloat16)

    def hop(chunk, row, k):
        block = pl.ds(row, ROWS), pl.ds(k * piece, piece)
        return pltpu.make_async_remote_copy(
            src_ref=down.at[block], dst_ref=up.at[block],
            send_sem=chain_send.at[chunk, k], recv_sem=chain_recv.at[chunk, k],
            device_id=onward, device_id_type=MESH,
        )

    def result(chunk, row):
        block = pl.ds(row, ROWS)
        return pltpu.make_async_copy(down.at[block], out_hbm.at[block], out_sem.at[chunk])

    def step(chunk, carry):
        micro, first, row, low, low_row = place_of(chunk)
        for k in range(KV_HEADS):

            @pl.when(section < sections - 1)
            def _():
                hop(chunk, row, k).wait_recv()

            heads = slice(k * HEAD_DIM, (k + 1) * HEAD_DIM)
            dv_heads = slice(width + k * HEAD_DIM, width + (k + 1) * HEAD_DIM)
            u = stacked(up, row, k)
            values = kv[pl.ds(low_row, WINDOW), dv_heads]
            dprobs = lax.dot_general(values, u, NT, preferred_element_type=jnp.float32)
            probs_rounded = pt[k]
            probs = probs_rounded.astype(jnp.float32)
            delta = jnp.sum(probs * dprobs, axis=0, keepdims=True)
            dscores = (probs * (dprobs - delta)).astype(jnp.bfloat16)
            acc[pl.ds(low_row, WINDOW), heads] += jnp.dot(
                dscores, stacked(q, row, k), preferred_element_type=jnp.float32
            )
            acc[pl.ds(low_row, WINDOW), dv_heads] += jnp.dot(
                probs_rounded, u, preferred_element_type=jnp.float32
            )
        dkeys = acc[pl.ds(row, ROWS), :width] * (1.0 / HEAD_DIM**0.5)
        dkv = jnp.concatenate([dkeys, acc[pl.ds(row, ROWS), width:]], axis=1).astype(jnp.bfloat16)
        for k in range(KV_HEADS):
            for owner in range(k * piece // shard, (k + 1) * piece // shard):
                cols = slice(owner * shard, (owner + 1) * shard)
                back = jnp.dot(dkv, wt[owner], preferred_element_type=jnp.float32)
                down[pl.ds(row, ROWS), cols] = (
                    up[pl.ds(row, ROWS), cols].astype(jnp.float32) + back
                ).astype(jnp.bfloat16)

            @pl.when(section > 0)
            def _():
                hop(chunk, row, k).start()

        result(chunk, row).start()

        @pl.when(chunk < chunks - 1)
        def _():
            scores(chunk + 1)

        return carry

    scores(0)

    @pl.when(section == sections - 1)
    def _():
        load_top.wait()

    lax.fori_loop(0, chunks, step, 0)

    def finish(chunk, carry):
        row = place_of(chunk)[2]
        result(chunk, row).wait()

        @pl.when(section > 0)
        def _():
            for k in range(KV_HEADS):
                hop(chunk, row, k).wait_send()

        return carry

    lax.fori_loop(0, chunks, finish, 0)
    for item in sent:
        copy(*item).wait_send()


def shards(inputs, queries, top_cotangent, key_weight, value_weight, order, doc_lengths):
    sections, fsdp = lax.axis_size("section"), lax.axis_size("fsdp")
    _, micros, tokens, features = inputs.shape
    shard, width = key_weight.shape[1:]
    rows = micros * tokens
    chunks = rows // ROWS
    bf16, f32 = jnp.bfloat16, jnp.float32
    hbm = pl.BlockSpec(memory_space=pl.ANY)
    grads = pl.pallas_call(
        functools.partial(kernel, sections, micros, tokens),
        out_shape=jax.ShapeDtypeStruct((rows, features), bf16),
        in_specs=[hbm] * 5 + [pl.BlockSpec(memory_space=pltpu.SMEM)],
        out_specs=hbm,
        scratch_shapes=[
            pltpu.VMEM((fsdp, 2 * width, shard), bf16),
            pltpu.VMEM((rows, features), bf16),
            pltpu.VMEM((rows, features), bf16),
            pltpu.VMEM((rows, features), bf16),
            pltpu.VMEM((rows, features), bf16),
            pltpu.VMEM((2, shard, width), bf16),
            pltpu.VMEM((rows, 2 * width), f32),
            pltpu.VMEM((rows, 2 * width), bf16),
            pltpu.VMEM((KV_HEADS, WINDOW, GROUP * ROWS), bf16),
            pltpu.VMEM((rows, 2 * width), f32),
            pltpu.SemaphoreType.DMA((5,)),
            pltpu.SemaphoreType.DMA((chunks,)),
            pltpu.SemaphoreType.DMA((15, 2)),
            pltpu.SemaphoreType.DMA((15, 2)),
            pltpu.SemaphoreType.DMA((chunks, KV_HEADS)),
            pltpu.SemaphoreType.DMA((chunks, KV_HEADS)),
        ],
        compiler_params=pltpu.CompilerParams(
            collective_id=0, has_side_effects=True, vmem_limit_bytes=52 << 20
        ),
        name="chain",
    )(
        inputs.reshape(rows, features),
        queries.reshape(rows, features),
        top_cotangent.reshape(rows, features),
        key_weight[0],
        value_weight[0],
        doc_lengths.reshape(micros, -1),
    )
    grads = grads.reshape(micros, tokens, features)
    return jnp.stack([lax.dynamic_index_in_dim(grads, order[k], 0, False) for k in range(micros)])[None]


def solution(mesh):
    placed = (
        P("section", None, "fsdp", None),
        P("section", None, "fsdp", None),
        P(None, "fsdp", None),
        P("section", "fsdp", None),
        P("section", "fsdp", None),
        P(),
        P(None, "fsdp", None),
    )
    return jax.shard_map(
        shards,
        mesh=mesh,
        in_specs=placed,
        out_specs=P("section", None, "fsdp", None),
        check_vma=False,
    )
```

```python
import functools
import math

import jax
import jax.numpy as jnp
from jax import lax
from jax.experimental import pallas as pl
from jax.experimental.pallas import tpu as pltpu
from jax.sharding import PartitionSpec as P

MESH = pl.DeviceIdType.MESH
HEADS = 64
KV_HEADS = 4
GROUP = HEADS // KV_HEADS
HEAD_DIM = 128
ROWS = 16
LONGEST = 64
WINDOW = LONGEST + ROWS
NT = (((1,), (1,)), ((), ()))


def kernel(
    sections, micros, tokens,
    acts_hbm, q_hbm, top_hbm, kw_hbm, vw_hbm, lens, down,
    wt, acts, q, up, raw, kv_acc, kv, pt, acc,
    load_sem, gather_send, gather_recv, chain_send, chain_recv,
):
    section, f = lax.axis_index("section"), lax.axis_index("fsdp")
    z, h, c = f // 4, (f // 2) % 2, f % 2
    shard = raw.shape[1]
    width = raw.shape[2]
    piece = GROUP * HEAD_DIM
    per_micro = tokens // ROWS
    chunks = micros * per_micro

    def index(dz, dh, dc):
        return 4 * ((z + dz + 4) % 4) + 2 * ((h + dh) % 2) + (c + dc) % 2

    z_next, z_prev = (section, index(1, 0, 0)), (section, index(-1, 0, 0))
    x_pair, core_pair = (section, index(0, 1, 0)), (section, index(0, 0, 1))
    onward = ((section + sections - 1) % sections, f)
    before = ((section + 1) % sections, f)

    loads = [
        pltpu.make_async_copy(kw_hbm, raw.at[0], load_sem.at[0]),
        pltpu.make_async_copy(vw_hbm, raw.at[1], load_sem.at[1]),
        pltpu.make_async_copy(acts_hbm, acts, load_sem.at[2]),
        pltpu.make_async_copy(q_hbm, q, load_sem.at[3]),
    ]
    load_top = pltpu.make_async_copy(top_hbm, up, load_sem.at[4])
    for load in loads[:2]:
        load.start()

    barrier = pltpu.get_barrier_semaphore()
    for device in (z_next, z_prev, x_pair, core_pair, onward, before):
        pl.semaphore_signal(barrier, inc=1, device_id=device, device_id_type=MESH)

    for part in range(2):
        loads[part].wait()
        wt[f, part * width:(part + 1) * width, :] = jnp.transpose(raw[part])
    pl.semaphore_wait(barrier, 6)

    places = [(0, 0), (-1, 0), (1, 0), (0, 1), (2, 0), (1, 1), (-1, 1), (2, 1)]
    third = (2 * width // 3) // 16 * 16
    parts = [(0, third), (third, third), (2 * third, 2 * width - 2 * third)]
    from_0, from_1, from_2 = (0, 1, 2), (1, 2, 0), (2, 0, 1)

    def copy(role, part, owner, device):
        first, size = parts[part]
        block = wt.at[owner, pl.ds(first, size), :]
        return pltpu.make_async_remote_copy(
            src_ref=block, dst_ref=block,
            send_sem=gather_send.at[role, part], recv_sem=gather_recv.at[role, part],
            device_id=device, device_id_type=MESH,
        )

    sent = []

    def send(role, part, place, device):
        owner = index(*places[place], 0)
        copy(role, part, owner, device).start()
        sent.append((role, part, owner, device))

    def arrive(role, part, place, device, dc=0):
        copy(role, part, index(*places[place], dc), device).wait_recv()

    def to_core(place, part):
        send(8 + place, part, place, core_pair)

    def add_keyval(place):
        for dc in range(2):
            if dc == 1:
                for part in from_0:
                    arrive(8 + place, part, place, core_pair, 1)
            owner = index(*places[place], dc)
            cols = pl.ds(pl.multiple_of(owner * shard, shard), shard)
            kv_acc[...] += lax.dot_general(
                acts[:, cols], wt[owner], NT, preferred_element_type=jnp.float32
            )

    for i in range(3):
        send(0, from_2[i], 0, z_next)
        send(1, from_0[i], 0, z_prev)
        send(2, from_1[i], 0, x_pair)
    for part in from_0:
        to_core(0, part)
    for load in loads[2:]:
        load.start()

    @pl.when(section == sections - 1)
    def _():
        load_top.start()

    kv_acc[...] = jnp.zeros_like(kv_acc)
    acc[...] = jnp.zeros_like(acc)
    for i in range(3):
        arrive(0, from_2[i], 1, z_prev)
        send(3, from_2[i], 1, z_next)
        if i > 0:
            send(4, from_0[i - 1], 1, x_pair)
        arrive(2, from_1[i], 3, x_pair)
        send(5, from_1[i], 3, z_prev)
        arrive(1, from_0[i], 2, z_next)
        to_core(1, from_2[i])
        to_core(3, from_1[i])
        to_core(2, from_0[i])
    send(4, from_0[2], 1, x_pair)
    for load in loads[2:]:
        load.wait()
    for place in (0, 1, 3, 2):
        add_keyval(place)
    for i in range(3):
        arrive(4, from_0[i], 6, x_pair)
        if i == 0:
            send(6, 0, 6, z_next)
        arrive(5, from_1[i], 5, z_next)
        if i == 0:
            send(6, 1, 5, z_prev)
        arrive(3, from_2[i], 4, z_prev)
        if i == 0:
            send(6, 2, 4, x_pair)
        to_core(6, from_0[i])
        to_core(5, from_1[i])
        to_core(4, from_2[i])
    for place in (6, 5, 4):
        add_keyval(place)
    for part, device in zip(from_0, (z_prev, z_next, x_pair)):
        arrive(6, part, 7, device)
        to_core(7, part)
    add_keyval(7)
    kv[...] = kv_acc[...].astype(jnp.bfloat16)

    def place_of(chunk):
        micro = chunk // per_micro
        first = tokens - ROWS - ROWS * (chunk % per_micro)
        base = micro * tokens
        row = pl.multiple_of(base + first, ROWS)
        low = jnp.maximum(first - LONGEST, 0)
        return micro, first, row, low, pl.multiple_of(base + low, ROWS)

    def stacked(ref, row, k):
        return jnp.concatenate(
            [
                ref[pl.ds(row, ROWS), (GROUP * k + g) * HEAD_DIM:(GROUP * k + g + 1) * HEAD_DIM]
                for g in range(GROUP)
            ],
            axis=0,
        )

    def scores(chunk):
        micro, first, row, low, low_row = place_of(chunk)
        end0 = lens[micro, 0, 0]
        end1 = end0 + lens[micro, 0, 1]
        end2 = end1 + lens[micro, 0, 2]
        shape = (WINDOW, GROUP * ROWS)
        i = first + lax.broadcasted_iota(jnp.int32, (1, shape[1]), 1) % ROWS
        begin = jnp.where(i >= end2, end2, jnp.where(i >= end1, end1, jnp.where(i >= end0, end0, 0)))
        j = low + lax.broadcasted_iota(jnp.int32, shape, 0)
        allowed = (j >= begin) & (j <= i)
        for k in range(KV_HEADS):
            keys = kv[pl.ds(low_row, WINDOW), k * HEAD_DIM:(k + 1) * HEAD_DIM]
            s = lax.dot_general(keys, stacked(q, row, k), NT, preferred_element_type=jnp.float32)
            s = jnp.where(allowed, s * (math.log2(math.e) / HEAD_DIM**0.5), -1e30)
            weights = jnp.exp2(s - jnp.max(s, axis=0, keepdims=True))
            probs = weights / jnp.sum(weights, axis=0, keepdims=True)
            pt[k] = probs.astype(jnp.bfloat16)

    def hop(chunk, row, k):
        block = pl.ds(row, ROWS), pl.ds(k * piece, piece)
        return pltpu.make_async_remote_copy(
            src_ref=down.at[block], dst_ref=up.at[block],
            send_sem=chain_send.at[chunk, k], recv_sem=chain_recv.at[chunk, k],
            device_id=onward, device_id_type=MESH,
        )

    def step(chunk, carry):
        micro, first, row, low, low_row = place_of(chunk)
        for k in range(KV_HEADS):

            @pl.when(section < sections - 1)
            def _():
                hop(chunk, row, k).wait_recv()

            heads = slice(k * HEAD_DIM, (k + 1) * HEAD_DIM)
            dv_heads = slice(width + k * HEAD_DIM, width + (k + 1) * HEAD_DIM)
            u = stacked(up, row, k)
            values = kv[pl.ds(low_row, WINDOW), dv_heads]
            dprobs = lax.dot_general(values, u, NT, preferred_element_type=jnp.float32)
            probs_rounded = pt[k]
            probs = probs_rounded.astype(jnp.float32)
            delta = jnp.sum(probs * dprobs, axis=0, keepdims=True)
            dscores = (probs * (dprobs - delta)).astype(jnp.bfloat16)
            acc[pl.ds(low_row, WINDOW), heads] += jnp.dot(
                dscores, stacked(q, row, k), preferred_element_type=jnp.float32
            )
            acc[pl.ds(low_row, WINDOW), dv_heads] += jnp.dot(
                probs_rounded, u, preferred_element_type=jnp.float32
            )
        dkeys = acc[pl.ds(row, ROWS), :width] * (1.0 / HEAD_DIM**0.5)
        dkv = jnp.concatenate([dkeys, acc[pl.ds(row, ROWS), width:]], axis=1).astype(jnp.bfloat16)
        for k in range(KV_HEADS):
            for owner in range(k * piece // shard, (k + 1) * piece // shard):
                cols = slice(owner * shard, (owner + 1) * shard)
                back = jnp.dot(dkv, wt[owner], preferred_element_type=jnp.float32)
                down[pl.ds(row, ROWS), cols] = (
                    up[pl.ds(row, ROWS), cols].astype(jnp.float32) + back
                ).astype(jnp.bfloat16)

            @pl.when(section > 0)
            def _():
                hop(chunk, row, k).start()

        @pl.when(chunk < chunks - 1)
        def _():
            scores(chunk + 1)

        return carry

    scores(0)

    @pl.when(section == sections - 1)
    def _():
        load_top.wait()

    lax.fori_loop(0, chunks, step, 0)

    def finish(chunk, carry):
        row = place_of(chunk)[2]
        @pl.when(section > 0)
        def _():
            for k in range(KV_HEADS):
                hop(chunk, row, k).wait_send()

        return carry

    lax.fori_loop(0, chunks, finish, 0)
    for item in sent:
        copy(*item).wait_send()


def place_micros(order, grads, out, sem):
    _, micros, tokens, _ = out.shape

    def copies():
        for k in range(micros):
            for i in range(tokens // ROWS):
                row = pl.multiple_of(order[k] * tokens + i * ROWS, ROWS)
                yield pltpu.make_async_copy(
                    grads.at[pl.ds(row, ROWS)], out.at[0, k, pl.ds(i * ROWS, ROWS)], sem.at[k, i]
                )

    for copy in copies():
        copy.start()
    for copy in copies():
        copy.wait()


def shards(inputs, queries, top_cotangent, key_weight, value_weight, order, doc_lengths):
    sections, fsdp = lax.axis_size("section"), lax.axis_size("fsdp")
    _, micros, tokens, features = inputs.shape
    shard, width = key_weight.shape[1:]
    rows = micros * tokens
    chunks = rows // ROWS
    bf16, f32 = jnp.bfloat16, jnp.float32
    hbm, vmem = pl.BlockSpec(memory_space=pl.ANY), pl.BlockSpec(memory_space=pltpu.VMEM)
    grads = pl.pallas_call(
        functools.partial(kernel, sections, micros, tokens),
        out_shape=pltpu.VMEM((rows, features), bf16),
        in_specs=[hbm] * 5 + [pl.BlockSpec(memory_space=pltpu.SMEM)],
        out_specs=vmem,
        scratch_shapes=[
            pltpu.VMEM((fsdp, 2 * width, shard), bf16),
            pltpu.VMEM((rows, features), bf16),
            pltpu.VMEM((rows, features), bf16),
            pltpu.VMEM((rows, features), bf16),
            pltpu.VMEM((2, shard, width), bf16),
            pltpu.VMEM((rows, 2 * width), f32),
            pltpu.VMEM((rows, 2 * width), bf16),
            pltpu.VMEM((KV_HEADS, WINDOW, GROUP * ROWS), bf16),
            pltpu.VMEM((rows, 2 * width), f32),
            pltpu.SemaphoreType.DMA((5,)),
            pltpu.SemaphoreType.DMA((16, 3)),
            pltpu.SemaphoreType.DMA((16, 3)),
            pltpu.SemaphoreType.DMA((chunks, KV_HEADS)),
            pltpu.SemaphoreType.DMA((chunks, KV_HEADS)),
        ],
        compiler_params=pltpu.CompilerParams(
            collective_id=0, has_side_effects=True, vmem_limit_bytes=56 << 20
        ),
        name="chain",
    )(
        inputs.reshape(rows, features),
        queries.reshape(rows, features),
        top_cotangent.reshape(rows, features),
        key_weight[0],
        value_weight[0],
        doc_lengths,
    )
    return pl.pallas_call(
        place_micros,
        out_shape=jax.ShapeDtypeStruct((1, micros, tokens, features), bf16),
        in_specs=[pl.BlockSpec(memory_space=pltpu.SMEM), vmem],
        out_specs=hbm,
        scratch_shapes=[pltpu.SemaphoreType.DMA((micros, tokens // ROWS))],
        compiler_params=pltpu.CompilerParams(vmem_limit_bytes=4 << 20),
        name="order",
    )(order, grads)


def solution(mesh):
    placed = (
        P("section", None, "fsdp", None),
        P("section", None, "fsdp", None),
        P(None, "fsdp", None),
        P("section", "fsdp", None),
        P("section", "fsdp", None),
        P(),
        P(None, "fsdp", None),
    )
    return jax.shard_map(
        shards,
        mesh=mesh,
        in_specs=placed,
        out_specs=P("section", None, "fsdp", None),
        check_vma=False,
    )
```

```python
import functools
import math

import jax
import jax.numpy as jnp
from jax import lax
from jax.experimental import pallas as pl
from jax.experimental.pallas import tpu as pltpu
from jax.sharding import PartitionSpec as P

MESH = pl.DeviceIdType.MESH
HEADS = 64
KV_HEADS = 4
GROUP = HEADS // KV_HEADS
HEAD_DIM = 128
ROWS = 16
LONGEST = 64
WINDOW = LONGEST + ROWS
NT = (((1,), (1,)), ((), ()))


def kernel(
    sections, micros, tokens,
    acts_hbm, q_hbm, top_hbm, kw_hbm, vw_hbm, lens, down,
    wt, relay, acts, q, up, raw, kv_acc, kv, pt, acc,
    load_sem, gather_send, gather_recv, chain_send, chain_recv,
):
    section, f = lax.axis_index("section"), lax.axis_index("fsdp")
    z, h, c = f // 4, (f // 2) % 2, f % 2
    shard = raw.shape[1]
    width = raw.shape[2]
    piece = GROUP * HEAD_DIM
    per_micro = tokens // ROWS
    chunks = micros * per_micro

    def index(dz, dh, dc):
        return 4 * ((z + dz + 4) % 4) + 2 * ((h + dh) % 2) + (c + dc) % 2

    z_next, z_prev = (section, index(1, 0, 0)), (section, index(-1, 0, 0))
    x_pair, core_pair = (section, index(0, 1, 0)), (section, index(0, 0, 1))
    onward = ((section + sections - 1) % sections, f)
    before = ((section + 1) % sections, f)

    loads = [
        pltpu.make_async_copy(kw_hbm, raw.at[0], load_sem.at[0]),
        pltpu.make_async_copy(vw_hbm, raw.at[1], load_sem.at[1]),
        pltpu.make_async_copy(acts_hbm, acts, load_sem.at[2]),
        pltpu.make_async_copy(q_hbm, q, load_sem.at[3]),
    ]
    load_top = pltpu.make_async_copy(top_hbm, up, load_sem.at[4])
    for load in loads[:2]:
        load.start()

    leading, helping = section >= sections - 2, section < 2
    opposite = (section + 2 * jnp.where(helping, sections // 2 - 1, 1)) % sections
    facing, across = (opposite, f), (opposite, index(2, 0, 0))
    barrier = pltpu.get_barrier_semaphore()
    for device in (z_next, z_prev, x_pair, core_pair, onward, before):
        pl.semaphore_signal(barrier, inc=1, device_id=device, device_id_type=MESH)

    @pl.when(leading | helping)
    def _():
        for device in (facing, across):
            pl.semaphore_signal(barrier, inc=1, device_id=device, device_id_type=MESH)

    for part in range(2):
        loads[part].wait()
        wt[f, part * width:(part + 1) * width, :] = jnp.transpose(raw[part])

    @pl.when(leading | helping)
    def _():
        pl.semaphore_wait(barrier, 8)

    @pl.when(jnp.logical_not(leading | helping))
    def _():
        pl.semaphore_wait(barrier, 6)

    places = [(0, 0), (-1, 0), (1, 0), (0, 1), (2, 0), (1, 1), (-1, 1), (2, 1)]
    third = (2 * width // 3) // 16 * 16
    parts = [(0, third), (third, third), (2 * third, 2 * width - 2 * third)]
    from_0, from_1, from_2 = (0, 1, 2), (1, 2, 0), (2, 0, 1)

    def copy(role, part, owner, device):
        first, size = parts[part]
        rows = pl.ds(first, size)
        source = relay.at[rows, :] if role == 17 else wt.at[owner, rows, :]
        target = relay.at[rows, :] if role == 16 else wt.at[owner, rows, :]
        return pltpu.make_async_remote_copy(
            src_ref=source, dst_ref=target,
            send_sem=gather_send.at[role, part], recv_sem=gather_recv.at[role, part],
            device_id=device, device_id_type=MESH,
        )

    owners = [index(*place, 0) for place in places]
    others = [index(*place, 1) for place in places]
    sent = {"all": [], "leading": [], "following": [], "helping": []}

    def send(role, part, place, device, who="all"):
        copy(role, part, owners[place], device).start()
        sent[who].append((role, part, owners[place], device))

    def arrive(role, part, place, device, dc=0):
        copy(role, part, (others if dc else owners)[place], device).wait_recv()

    def to_core(place, part, who="all"):
        send(8 + place, part, place, core_pair, who)

    def add_keyval(place):
        for dc in range(2):
            if dc == 1:
                for part in from_0:
                    arrive(8 + place, part, place, core_pair, 1)
            owner = (others if dc else owners)[place]
            cols = pl.ds(pl.multiple_of(owner * shard, shard), shard)
            kv_acc[...] += lax.dot_general(
                acts[:, cols], wt[owner], NT, preferred_element_type=jnp.float32
            )

    for load in loads[2:]:
        load.start()

    @pl.when(section == sections - 1)
    def _():
        load_top.start()

    @pl.when(leading)
    def _():
        for part in from_0:
            send(16, part, 0, across, "leading")

    @pl.when(helping)
    def _():
        for part in from_0:
            arrive(16, part, 0, across)
            send(17, part, 4, facing, "helping")

    for i in range(3):
        send(0, from_2[i], 0, z_next)
        send(1, from_0[i], 0, z_prev)
        send(2, from_1[i], 0, x_pair)
    for part in from_0:
        to_core(0, part)
    kv_acc[...] = jnp.zeros_like(kv_acc)
    acc[...] = jnp.zeros_like(acc)
    for i in range(3):
        arrive(0, from_2[i], 1, z_prev)

        @pl.when(jnp.logical_not(leading))
        def _():
            send(3, from_2[i], 1, z_next, "following")
            if i > 0:
                send(4, from_0[i - 1], 1, x_pair, "following")

        arrive(2, from_1[i], 3, x_pair)

        @pl.when(leading)
        def _():
            send(3, from_1[i], 3, z_next, "leading")

        send(5, from_1[i], 3, z_prev)
        arrive(1, from_0[i], 2, z_next)
        to_core(1, from_2[i])
        to_core(3, from_1[i])
        to_core(2, from_0[i])

    @pl.when(jnp.logical_not(leading))
    def _():
        send(4, from_0[2], 1, x_pair, "following")

    def relayed(part):
        @pl.when(leading)
        def _():
            arrive(17, part, 4, facing)
            send(4, part, 4, x_pair, "leading")
            to_core(4, part, "leading")

    relayed(0)
    for load in loads[2:]:
        load.wait()
    add_keyval(0)
    add_keyval(1)
    relayed(1)
    add_keyval(3)
    add_keyval(2)
    relayed(2)

    @pl.when(jnp.logical_not(leading))
    def _():
        for i in range(3):
            arrive(4, from_0[i], 6, x_pair)
            if i == 0:
                send(6, 0, 6, z_next, "following")
            arrive(5, from_1[i], 5, z_next)
            if i == 0:
                send(6, 1, 5, z_prev, "following")
            arrive(3, from_2[i], 4, z_prev)
            if i == 0:
                send(6, 2, 4, x_pair, "following")
            to_core(6, from_0[i], "following")
            to_core(5, from_1[i], "following")
            to_core(4, from_2[i], "following")

    @pl.when(leading)
    def _():
        for i in range(3):
            arrive(3, from_1[i], 6, z_prev)
            to_core(6, from_1[i], "leading")
            arrive(5, from_1[i], 5, z_next)
            to_core(5, from_1[i], "leading")

    for place in (4, 6, 5):
        add_keyval(place)

    @pl.when(jnp.logical_not(leading))
    def _():
        for part, device in zip(from_0, (z_prev, z_next, x_pair)):
            arrive(6, part, 7, device)
            to_core(7, part, "following")

    @pl.when(leading)
    def _():
        for part in from_0:
            arrive(4, part, 7, x_pair)
            to_core(7, part, "leading")

    add_keyval(7)
    kv[...] = kv_acc[...].astype(jnp.bfloat16)

    def place_of(chunk):
        micro = chunk // per_micro
        first = tokens - ROWS - ROWS * (chunk % per_micro)
        base = micro * tokens
        row = pl.multiple_of(base + first, ROWS)
        low = jnp.maximum(first - LONGEST, 0)
        return micro, first, row, low, pl.multiple_of(base + low, ROWS)

    def stacked(ref, row, k):
        return jnp.concatenate(
            [
                ref[pl.ds(row, ROWS), (GROUP * k + g) * HEAD_DIM:(GROUP * k + g + 1) * HEAD_DIM]
                for g in range(GROUP)
            ],
            axis=0,
        )

    def scores(chunk):
        micro, first, row, low, low_row = place_of(chunk)
        end0 = lens[micro, 0, 0]
        end1 = end0 + lens[micro, 0, 1]
        end2 = end1 + lens[micro, 0, 2]
        shape = (WINDOW, GROUP * ROWS)
        i = first + lax.broadcasted_iota(jnp.int32, (1, shape[1]), 1) % ROWS
        begin = jnp.where(i >= end2, end2, jnp.where(i >= end1, end1, jnp.where(i >= end0, end0, 0)))
        j = low + lax.broadcasted_iota(jnp.int32, shape, 0)
        allowed = (j >= begin) & (j <= i)
        for k in range(KV_HEADS):
            keys = kv[pl.ds(low_row, WINDOW), k * HEAD_DIM:(k + 1) * HEAD_DIM]
            s = lax.dot_general(keys, stacked(q, row, k), NT, preferred_element_type=jnp.float32)
            s = jnp.where(allowed, s * (math.log2(math.e) / HEAD_DIM**0.5), -1e30)
            weights = jnp.exp2(s - jnp.max(s, axis=0, keepdims=True))
            probs = weights / jnp.sum(weights, axis=0, keepdims=True)
            pt[k] = probs.astype(jnp.bfloat16)

    def hop(chunk, row, k):
        block = pl.ds(row, ROWS), pl.ds(k * piece, piece)
        return pltpu.make_async_remote_copy(
            src_ref=down.at[block], dst_ref=up.at[block],
            send_sem=chain_send.at[chunk, k], recv_sem=chain_recv.at[chunk, k],
            device_id=onward, device_id_type=MESH,
        )

    def step(chunk, carry):
        micro, first, row, low, low_row = place_of(chunk)
        for group in ((0, 1, 2), (3,)):

            @pl.when(section < sections - 1)
            def _():
                for k in group:
                    hop(chunk, row, k).wait_recv()

            for k in group:
                heads = slice(k * HEAD_DIM, (k + 1) * HEAD_DIM)
                dv_heads = slice(width + k * HEAD_DIM, width + (k + 1) * HEAD_DIM)
                u = stacked(up, row, k)
                values = kv[pl.ds(low_row, WINDOW), dv_heads]
                dprobs = lax.dot_general(values, u, NT, preferred_element_type=jnp.float32)
                probs_rounded = pt[k]
                probs = probs_rounded.astype(jnp.float32)
                delta = jnp.sum(probs * dprobs, axis=0, keepdims=True)
                dscores = (probs * (dprobs - delta)).astype(jnp.bfloat16)
                acc[pl.ds(low_row, WINDOW), heads] += jnp.dot(
                    dscores, stacked(q, row, k), preferred_element_type=jnp.float32
                )
                acc[pl.ds(low_row, WINDOW), dv_heads] += jnp.dot(
                    probs_rounded, u, preferred_element_type=jnp.float32
                )
        dkeys = acc[pl.ds(row, ROWS), :width] * (1.0 / HEAD_DIM**0.5)
        dkv = jnp.concatenate([dkeys, acc[pl.ds(row, ROWS), width:]], axis=1).astype(jnp.bfloat16)
        for k in range(KV_HEADS):
            for owner in range(k * piece // shard, (k + 1) * piece // shard):
                cols = slice(owner * shard, (owner + 1) * shard)
                back = jnp.dot(dkv, wt[owner], preferred_element_type=jnp.float32)
                down[pl.ds(row, ROWS), cols] = (
                    up[pl.ds(row, ROWS), cols].astype(jnp.float32) + back
                ).astype(jnp.bfloat16)

            @pl.when(section > 0)
            def _():
                hop(chunk, row, k).start()

        @pl.when(chunk < chunks - 1)
        def _():
            scores(chunk + 1)

        return carry

    scores(0)

    @pl.when(section == sections - 1)
    def _():
        load_top.wait()

    lax.fori_loop(0, chunks, step, 0)

    def finish(chunk, carry):
        row = place_of(chunk)[2]
        @pl.when(section > 0)
        def _():
            for k in range(KV_HEADS):
                hop(chunk, row, k).wait_send()

        return carry

    lax.fori_loop(0, chunks, finish, 0)
    def all_sent(who):
        for item in sent[who]:
            copy(*item).wait_send()

    all_sent("all")
    pl.when(leading)(lambda: all_sent("leading"))
    pl.when(jnp.logical_not(leading))(lambda: all_sent("following"))
    pl.when(helping)(lambda: all_sent("helping"))


def place_micros(order, grads, out, sem):
    _, micros, tokens, _ = out.shape

    def copies():
        for k in range(micros):
            for i in range(tokens // ROWS):
                row = pl.multiple_of(order[k] * tokens + i * ROWS, ROWS)
                yield pltpu.make_async_copy(
                    grads.at[pl.ds(row, ROWS)], out.at[0, k, pl.ds(i * ROWS, ROWS)], sem.at[k, i]
                )

    for copy in copies():
        copy.start()
    for copy in copies():
        copy.wait()


def shards(inputs, queries, top_cotangent, key_weight, value_weight, order, doc_lengths):
    sections, fsdp = lax.axis_size("section"), lax.axis_size("fsdp")
    _, micros, tokens, features = inputs.shape
    shard, width = key_weight.shape[1:]
    rows = micros * tokens
    chunks = rows // ROWS
    bf16, f32 = jnp.bfloat16, jnp.float32
    hbm, vmem = pl.BlockSpec(memory_space=pl.ANY), pl.BlockSpec(memory_space=pltpu.VMEM)
    grads = pl.pallas_call(
        functools.partial(kernel, sections, micros, tokens),
        out_shape=pltpu.VMEM((rows, features), bf16),
        in_specs=[hbm] * 5 + [pl.BlockSpec(memory_space=pltpu.SMEM)],
        out_specs=vmem,
        scratch_shapes=[
            pltpu.VMEM((fsdp, 2 * width, shard), bf16),
            pltpu.VMEM((2 * width, shard), bf16),
            pltpu.VMEM((rows, features), bf16),
            pltpu.VMEM((rows, features), bf16),
            pltpu.VMEM((rows, features), bf16),
            pltpu.VMEM((2, shard, width), bf16),
            pltpu.VMEM((rows, 2 * width), f32),
            pltpu.VMEM((rows, 2 * width), bf16),
            pltpu.VMEM((KV_HEADS, WINDOW, GROUP * ROWS), bf16),
            pltpu.VMEM((rows, 2 * width), f32),
            pltpu.SemaphoreType.DMA((5,)),
            pltpu.SemaphoreType.DMA((18, 3)),
            pltpu.SemaphoreType.DMA((18, 3)),
            pltpu.SemaphoreType.DMA((chunks, KV_HEADS)),
            pltpu.SemaphoreType.DMA((chunks, KV_HEADS)),
        ],
        compiler_params=pltpu.CompilerParams(
            collective_id=0, has_side_effects=True, vmem_limit_bytes=56 << 20
        ),
        name="chain",
    )(
        inputs.reshape(rows, features),
        queries.reshape(rows, features),
        top_cotangent.reshape(rows, features),
        key_weight[0],
        value_weight[0],
        doc_lengths,
    )
    return pl.pallas_call(
        place_micros,
        out_shape=jax.ShapeDtypeStruct((1, micros, tokens, features), bf16),
        in_specs=[pl.BlockSpec(memory_space=pltpu.SMEM), vmem],
        out_specs=hbm,
        scratch_shapes=[pltpu.SemaphoreType.DMA((micros, tokens // ROWS))],
        compiler_params=pltpu.CompilerParams(vmem_limit_bytes=4 << 20),
        name="order",
    )(order, grads)


def solution(mesh):
    placed = (
        P("section", None, "fsdp", None),
        P("section", None, "fsdp", None),
        P(None, "fsdp", None),
        P("section", "fsdp", None),
        P("section", "fsdp", None),
        P(),
        P(None, "fsdp", None),
    )
    return jax.shard_map(
        shards,
        mesh=mesh,
        in_specs=placed,
        out_specs=P("section", None, "fsdp", None),
        check_vma=False,
    )
```

```python
import functools
import math

import jax
import jax.numpy as jnp
from jax import lax
from jax.experimental import pallas as pl
from jax.experimental.pallas import tpu as pltpu
from jax.sharding import PartitionSpec as P

MESH = pl.DeviceIdType.MESH
HEADS = 64
KV_HEADS = 4
GROUP = HEADS // KV_HEADS
HEAD_DIM = 128
ROWS = 16
LONGEST = 64
WINDOW = LONGEST + ROWS
NT = (((1,), (1,)), ((), ()))


def kernel(
    sections, micros, tokens,
    acts_hbm, q_hbm, top_hbm, kw_hbm, vw_hbm, lens, down,
    wt, relay, acts, q, up, raw, kv_acc, kv, pt, acc, total,
    load_sem, gather_send, gather_recv, chain_send, chain_recv,
):
    section, f = lax.axis_index("section"), lax.axis_index("fsdp")
    z, h, c = f // 4, (f // 2) % 2, f % 2
    shard = raw.shape[1]
    width = raw.shape[2]
    piece = GROUP * HEAD_DIM
    per_micro = tokens // ROWS
    chunks = micros * per_micro

    def index(dz, dh, dc):
        return 4 * ((z + dz + 4) % 4) + 2 * ((h + dh) % 2) + (c + dc) % 2

    z_next, z_prev = (section, index(1, 0, 0)), (section, index(-1, 0, 0))
    x_pair, core_pair = (section, index(0, 1, 0)), (section, index(0, 0, 1))
    onward = ((section + sections - 1) % sections, f)
    before = ((section + 1) % sections, f)

    loads = [
        pltpu.make_async_copy(kw_hbm, raw.at[0], load_sem.at[0]),
        pltpu.make_async_copy(vw_hbm, raw.at[1], load_sem.at[1]),
        pltpu.make_async_copy(acts_hbm, acts, load_sem.at[2]),
        pltpu.make_async_copy(q_hbm, q, load_sem.at[3]),
    ]
    load_top = pltpu.make_async_copy(top_hbm, up, load_sem.at[4])
    for load in loads[:2]:
        load.start()

    leading, helping = section >= sections - 2, section < 2
    opposite = (section + 2 * jnp.where(helping, sections // 2 - 1, 1)) % sections
    facing, across = (opposite, f), (opposite, index(2, 0, 0))
    barrier = pltpu.get_barrier_semaphore()
    for device in (z_next, z_prev, x_pair, core_pair, onward, before):
        pl.semaphore_signal(barrier, inc=1, device_id=device, device_id_type=MESH)

    @pl.when(leading | helping)
    def _():
        for device in (facing, across):
            pl.semaphore_signal(barrier, inc=1, device_id=device, device_id_type=MESH)

    for part in range(2):
        loads[part].wait()
        wt[f, part * width:(part + 1) * width, :] = jnp.transpose(raw[part])

    @pl.when(leading | helping)
    def _():
        pl.semaphore_wait(barrier, 8)

    @pl.when(jnp.logical_not(leading | helping))
    def _():
        pl.semaphore_wait(barrier, 6)

    places = [(0, 0), (-1, 0), (1, 0), (0, 1), (2, 0), (1, 1), (-1, 1), (2, 1)]
    third = (2 * width // 3) // 16 * 16
    parts = [(0, third), (third, third), (2 * third, 2 * width - 2 * third)]
    from_0, from_1, from_2 = (0, 1, 2), (1, 2, 0), (2, 0, 1)

    def copy(role, part, owner, device):
        first, size = parts[part]
        rows = pl.ds(first, size)
        source = relay.at[rows, :] if role == 17 else wt.at[owner, rows, :]
        target = relay.at[rows, :] if role == 16 else wt.at[owner, rows, :]
        return pltpu.make_async_remote_copy(
            src_ref=source, dst_ref=target,
            send_sem=gather_send.at[role, part], recv_sem=gather_recv.at[role, part],
            device_id=device, device_id_type=MESH,
        )

    owners = [index(*place, 0) for place in places]
    others = [index(*place, 1) for place in places]
    sent = {"all": [], "leading": [], "following": [], "helping": []}

    def send(role, part, place, device, who="all"):
        copy(role, part, owners[place], device).start()
        sent[who].append((role, part, owners[place], device))

    def arrive(role, part, place, device, dc=0):
        copy(role, part, (others if dc else owners)[place], device).wait_recv()

    def to_core(place, part, who="all"):
        send(8 + place, part, place, core_pair, who)

    def add_keyval(place):
        for dc in range(2):
            if dc == 1:
                for part in from_0:
                    arrive(8 + place, part, place, core_pair, 1)
            owner = (others if dc else owners)[place]
            cols = pl.ds(pl.multiple_of(owner * shard, shard), shard)
            kv_acc[...] += lax.dot_general(
                acts[:, cols], wt[owner], NT, preferred_element_type=jnp.float32
            )

    for load in loads[2:]:
        load.start()

    @pl.when(section == sections - 1)
    def _():
        load_top.start()

    @pl.when(leading)
    def _():
        for part in from_0:
            send(16, part, 0, across, "leading")

    @pl.when(helping)
    def _():
        for part in from_0:
            arrive(16, part, 0, across)
            send(17, part, 4, facing, "helping")

    for i in range(3):
        send(0, from_2[i], 0, z_next)
        send(1, from_0[i], 0, z_prev)
        send(2, from_1[i], 0, x_pair)
    for part in from_0:
        to_core(0, part)
    kv_acc[...] = jnp.zeros_like(kv_acc)
    acc[...] = jnp.zeros_like(acc)
    for i in range(3):
        arrive(0, from_2[i], 1, z_prev)

        @pl.when(jnp.logical_not(leading))
        def _():
            send(3, from_2[i], 1, z_next, "following")
            if i > 0:
                send(4, from_0[i - 1], 1, x_pair, "following")

        arrive(2, from_1[i], 3, x_pair)

        @pl.when(leading)
        def _():
            send(3, from_1[i], 3, z_next, "leading")

        send(5, from_1[i], 3, z_prev)
        arrive(1, from_0[i], 2, z_next)
        to_core(1, from_2[i])
        to_core(3, from_1[i])
        to_core(2, from_0[i])

    @pl.when(jnp.logical_not(leading))
    def _():
        send(4, from_0[2], 1, x_pair, "following")

    def relayed(part):
        @pl.when(leading)
        def _():
            arrive(17, part, 4, facing)
            send(4, part, 4, x_pair, "leading")
            to_core(4, part, "leading")

    relayed(0)
    for load in loads[2:]:
        load.wait()
    add_keyval(0)
    add_keyval(1)
    relayed(1)
    add_keyval(3)
    add_keyval(2)
    relayed(2)

    @pl.when(jnp.logical_not(leading))
    def _():
        for i in range(3):
            arrive(4, from_0[i], 6, x_pair)
            if i == 0:
                send(6, 0, 6, z_next, "following")
            arrive(5, from_1[i], 5, z_next)
            if i == 0:
                send(6, 1, 5, z_prev, "following")
            arrive(3, from_2[i], 4, z_prev)
            if i == 0:
                send(6, 2, 4, x_pair, "following")
            to_core(6, from_0[i], "following")
            to_core(5, from_1[i], "following")
            to_core(4, from_2[i], "following")

    @pl.when(leading)
    def _():
        for i in range(3):
            arrive(3, from_1[i], 6, z_prev)
            to_core(6, from_1[i], "leading")
            arrive(5, from_1[i], 5, z_next)
            to_core(5, from_1[i], "leading")

    for place in (4, 6, 5):
        add_keyval(place)

    @pl.when(jnp.logical_not(leading))
    def _():
        for part, device in zip(from_0, (z_prev, z_next, x_pair)):
            arrive(6, part, 7, device)
            to_core(7, part, "following")

    @pl.when(leading)
    def _():
        for part in from_0:
            arrive(4, part, 7, x_pair)
            to_core(7, part, "leading")

    add_keyval(7)
    kv[...] = kv_acc[...].astype(jnp.bfloat16)

    def place_of(chunk):
        micro = chunk // per_micro
        first = tokens - ROWS - ROWS * (chunk % per_micro)
        base = micro * tokens
        row = pl.multiple_of(base + first, ROWS)
        low = jnp.maximum(first - LONGEST, 0)
        return micro, first, row, low, pl.multiple_of(base + low, ROWS)

    def stacked(ref, row, k):
        return jnp.concatenate(
            [
                ref[pl.ds(row, ROWS), (GROUP * k + g) * HEAD_DIM:(GROUP * k + g + 1) * HEAD_DIM]
                for g in range(GROUP)
            ],
            axis=0,
        )

    def scores(chunk):
        micro, first, row, low, low_row = place_of(chunk)
        end0 = lens[micro, 0, 0]
        end1 = end0 + lens[micro, 0, 1]
        end2 = end1 + lens[micro, 0, 2]
        shape = (WINDOW, GROUP * ROWS)
        i = first + lax.broadcasted_iota(jnp.int32, (1, shape[1]), 1) % ROWS
        begin = jnp.where(i >= end2, end2, jnp.where(i >= end1, end1, jnp.where(i >= end0, end0, 0)))
        j = low + lax.broadcasted_iota(jnp.int32, shape, 0)
        allowed = (j >= begin) & (j <= i)
        for k in range(KV_HEADS):
            keys = kv[pl.ds(low_row, WINDOW), k * HEAD_DIM:(k + 1) * HEAD_DIM]
            s = lax.dot_general(keys, stacked(q, row, k), NT, preferred_element_type=jnp.float32)
            s = jnp.where(allowed, s * (math.log2(math.e) / HEAD_DIM**0.5), -1e30)
            weights = jnp.exp2(s - jnp.max(s, axis=0, keepdims=True))
            probs = weights / jnp.sum(weights, axis=0, keepdims=True)
            pt[k] = probs.astype(jnp.bfloat16)

    def hop(chunk, row, k):
        block = pl.ds(row, ROWS), pl.ds(k * piece, piece)
        return pltpu.make_async_remote_copy(
            src_ref=down.at[block], dst_ref=up.at[block],
            send_sem=chain_send.at[chunk, k], recv_sem=chain_recv.at[chunk, k],
            device_id=onward, device_id_type=MESH,
        )

    def step(chunk, carry):
        micro, first, row, low, low_row = place_of(chunk)
        def attend(k):
            heads = slice(k * HEAD_DIM, (k + 1) * HEAD_DIM)
            dv_heads = slice(width + k * HEAD_DIM, width + (k + 1) * HEAD_DIM)
            u = stacked(up, row, k)
            values = kv[pl.ds(low_row, WINDOW), dv_heads]
            dprobs = lax.dot_general(values, u, NT, preferred_element_type=jnp.float32)
            probs_rounded = pt[k]
            probs = probs_rounded.astype(jnp.float32)
            delta = jnp.sum(probs * dprobs, axis=0, keepdims=True)
            dscores = (probs * (dprobs - delta)).astype(jnp.bfloat16)
            acc[pl.ds(low_row, WINDOW), heads] += jnp.dot(
                dscores, stacked(q, row, k), preferred_element_type=jnp.float32
            )
            acc[pl.ds(low_row, WINDOW), dv_heads] += jnp.dot(
                probs_rounded, u, preferred_element_type=jnp.float32
            )

        @pl.when(section == sections - 1)
        def _():
            for k in range(KV_HEADS):
                attend(k)
            dkeys = acc[pl.ds(row, ROWS), :width] * (1.0 / HEAD_DIM**0.5)
            dkv = jnp.concatenate([dkeys, acc[pl.ds(row, ROWS), width:]], axis=1).astype(jnp.bfloat16)
            for k in range(KV_HEADS):
                for owner in range(k * piece // shard, (k + 1) * piece // shard):
                    cols = slice(owner * shard, (owner + 1) * shard)
                    back = jnp.dot(dkv, wt[owner], preferred_element_type=jnp.float32)
                    down[pl.ds(row, ROWS), cols] = (
                        up[pl.ds(row, ROWS), cols].astype(jnp.float32) + back
                    ).astype(jnp.bfloat16)
                hop(chunk, row, k).start()

        @pl.when(section < sections - 1)
        def _():
            for k in range(KV_HEADS):
                hop(chunk, row, k).wait_recv()
                attend(k)
                heads = slice(k * HEAD_DIM, (k + 1) * HEAD_DIM)
                dv_heads = slice(width + k * HEAD_DIM, width + (k + 1) * HEAD_DIM)
                dkeys = acc[pl.ds(row, ROWS), heads] * (1.0 / HEAD_DIM**0.5)
                dkv = jnp.concatenate([dkeys, acc[pl.ds(row, ROWS), dv_heads]], axis=1).astype(jnp.bfloat16)
                for owner in range(wt.shape[0]):
                    cols = slice(owner * shard, (owner + 1) * shard)
                    weights = jnp.concatenate([wt[owner, heads, :], wt[owner, dv_heads, :]], axis=0)
                    back = jnp.dot(dkv, weights, preferred_element_type=jnp.float32)
                    if owner * shard // piece == k:
                        back += up[pl.ds(row, ROWS), cols].astype(jnp.float32)
                    if k > 0:
                        back += total[:, cols]
                    if k < KV_HEADS - 1:
                        total[:, cols] = back
                    else:
                        down[pl.ds(row, ROWS), cols] = back.astype(jnp.bfloat16)
                    done, rest = divmod((owner + 1) * shard, piece)
                    if k == KV_HEADS - 1 and rest == 0:

                        @pl.when(section > 0)
                        def _():
                            hop(chunk, row, done - 1).start()

        @pl.when(chunk < chunks - 1)
        def _():
            scores(chunk + 1)

        return carry

    scores(0)

    @pl.when(section == sections - 1)
    def _():
        load_top.wait()

    lax.fori_loop(0, chunks, step, 0)

    def finish(chunk, carry):
        row = place_of(chunk)[2]
        @pl.when(section > 0)
        def _():
            for k in range(KV_HEADS):
                hop(chunk, row, k).wait_send()

        return carry

    lax.fori_loop(0, chunks, finish, 0)
    def all_sent(who):
        for item in sent[who]:
            copy(*item).wait_send()

    all_sent("all")
    pl.when(leading)(lambda: all_sent("leading"))
    pl.when(jnp.logical_not(leading))(lambda: all_sent("following"))
    pl.when(helping)(lambda: all_sent("helping"))


def place_micros(order, grads, out, sem):
    _, micros, tokens, _ = out.shape

    def copies():
        for k in range(micros):
            for i in range(tokens // ROWS):
                row = pl.multiple_of(order[k] * tokens + i * ROWS, ROWS)
                yield pltpu.make_async_copy(
                    grads.at[pl.ds(row, ROWS)], out.at[0, k, pl.ds(i * ROWS, ROWS)], sem.at[k, i]
                )

    for copy in copies():
        copy.start()
    for copy in copies():
        copy.wait()


def shards(inputs, queries, top_cotangent, key_weight, value_weight, order, doc_lengths):
    sections, fsdp = lax.axis_size("section"), lax.axis_size("fsdp")
    _, micros, tokens, features = inputs.shape
    shard, width = key_weight.shape[1:]
    rows = micros * tokens
    chunks = rows // ROWS
    bf16, f32 = jnp.bfloat16, jnp.float32
    hbm, vmem = pl.BlockSpec(memory_space=pl.ANY), pl.BlockSpec(memory_space=pltpu.VMEM)
    grads = pl.pallas_call(
        functools.partial(kernel, sections, micros, tokens),
        out_shape=pltpu.VMEM((rows, features), bf16),
        in_specs=[hbm] * 5 + [pl.BlockSpec(memory_space=pltpu.SMEM)],
        out_specs=vmem,
        scratch_shapes=[
            pltpu.VMEM((fsdp, 2 * width, shard), bf16),
            pltpu.VMEM((2 * width, shard), bf16),
            pltpu.VMEM((rows, features), bf16),
            pltpu.VMEM((rows, features), bf16),
            pltpu.VMEM((rows, features), bf16),
            pltpu.VMEM((2, shard, width), bf16),
            pltpu.VMEM((rows, 2 * width), f32),
            pltpu.VMEM((rows, 2 * width), bf16),
            pltpu.VMEM((KV_HEADS, WINDOW, GROUP * ROWS), bf16),
            pltpu.VMEM((rows, 2 * width), f32),
            pltpu.VMEM((ROWS, features), f32),
            pltpu.SemaphoreType.DMA((5,)),
            pltpu.SemaphoreType.DMA((18, 3)),
            pltpu.SemaphoreType.DMA((18, 3)),
            pltpu.SemaphoreType.DMA((chunks, KV_HEADS)),
            pltpu.SemaphoreType.DMA((chunks, KV_HEADS)),
        ],
        compiler_params=pltpu.CompilerParams(
            collective_id=0, has_side_effects=True, vmem_limit_bytes=56 << 20
        ),
        name="chain",
    )(
        inputs.reshape(rows, features),
        queries.reshape(rows, features),
        top_cotangent.reshape(rows, features),
        key_weight[0],
        value_weight[0],
        doc_lengths,
    )
    return pl.pallas_call(
        place_micros,
        out_shape=jax.ShapeDtypeStruct((1, micros, tokens, features), bf16),
        in_specs=[pl.BlockSpec(memory_space=pltpu.SMEM), vmem],
        out_specs=hbm,
        scratch_shapes=[pltpu.SemaphoreType.DMA((micros, tokens // ROWS))],
        compiler_params=pltpu.CompilerParams(vmem_limit_bytes=4 << 20),
        name="order",
    )(order, grads)


def solution(mesh):
    placed = (
        P("section", None, "fsdp", None),
        P("section", None, "fsdp", None),
        P(None, "fsdp", None),
        P("section", "fsdp", None),
        P("section", "fsdp", None),
        P(),
        P(None, "fsdp", None),
    )
    return jax.shard_map(
        shards,
        mesh=mesh,
        in_specs=placed,
        out_specs=P("section", None, "fsdp", None),
        check_vma=False,
    )
```

```python
import functools
import math

import jax
import jax.numpy as jnp
from jax import lax
from jax.experimental import pallas as pl
from jax.experimental.pallas import tpu as pltpu
from jax.sharding import PartitionSpec as P

MESH = pl.DeviceIdType.MESH
HEADS = 64
KV_HEADS = 4
GROUP = HEADS // KV_HEADS
HEAD_DIM = 128
ROWS = 16
LONGEST = 64
WINDOW = LONGEST + ROWS
NT = (((1,), (1,)), ((), ()))


def kernel(
    sections, micros, tokens,
    acts_hbm, q_hbm, top_hbm, kw_hbm, vw_hbm, lens, down,
    wt, relay, acts, q, up, raw, kv_acc, kv, pt, acc, total,
    load_sem, gather_send, gather_recv, chain_send, chain_recv, turn,
):
    section, f = lax.axis_index("section"), lax.axis_index("fsdp")
    z, h, c = f // 4, (f // 2) % 2, f % 2
    shard = raw.shape[1]
    width = raw.shape[2]
    piece = GROUP * HEAD_DIM
    per_micro = tokens // ROWS
    chunks = micros * per_micro

    def index(dz, dh, dc):
        return 4 * ((z + dz + 4) % 4) + 2 * ((h + dh) % 2) + (c + dc) % 2

    z_next, z_prev = (section, index(1, 0, 0)), (section, index(-1, 0, 0))
    x_pair, core_pair = (section, index(0, 1, 0)), (section, index(0, 0, 1))
    onward = ((section + sections - 1) % sections, f)
    before = ((section + 1) % sections, f)

    loads = [
        pltpu.make_async_copy(kw_hbm, raw.at[0], load_sem.at[0]),
        pltpu.make_async_copy(vw_hbm, raw.at[1], load_sem.at[1]),
        pltpu.make_async_copy(acts_hbm, acts, load_sem.at[2]),
        pltpu.make_async_copy(q_hbm, q, load_sem.at[3]),
    ]
    load_top = pltpu.make_async_copy(top_hbm, up, load_sem.at[4])
    for load in loads[:2]:
        load.start()

    leading, helping = section >= sections - 2, section < 2
    opposite = (section + 2 * jnp.where(helping, sections // 2 - 1, 1)) % sections
    facing, across = (opposite, f), (opposite, index(2, 0, 0))
    barrier = pltpu.get_barrier_semaphore()
    for device in (z_next, z_prev, x_pair, core_pair, onward, before):
        pl.semaphore_signal(barrier, inc=1, device_id=device, device_id_type=MESH)

    @pl.when(leading | helping)
    def _():
        for device in (facing, across):
            pl.semaphore_signal(barrier, inc=1, device_id=device, device_id_type=MESH)

    for part in range(2):
        loads[part].wait()
        wt[f, part * width:(part + 1) * width, :] = jnp.transpose(raw[part])

    @pl.when(leading | helping)
    def _():
        pl.semaphore_wait(barrier, 8)

    @pl.when(jnp.logical_not(leading | helping))
    def _():
        pl.semaphore_wait(barrier, 6)

    places = [(0, 0), (-1, 0), (1, 0), (0, 1), (2, 0), (1, 1), (-1, 1), (2, 1)]
    third = 3 * width // 4
    parts = [(0, 2 * width - 2 * third), (2 * width - 2 * third, third), (2 * width - third, third)]
    from_0, from_1, from_2 = (0, 1, 2), (1, 2, 0), (2, 0, 1)

    def copy(role, part, owner, device):
        first, size = parts[part]
        rows = pl.ds(first, size)
        source = relay.at[rows, :] if role == 17 else wt.at[owner, rows, :]
        target = relay.at[rows, :] if role == 16 else wt.at[owner, rows, :]
        return pltpu.make_async_remote_copy(
            src_ref=source, dst_ref=target,
            send_sem=gather_send.at[role, part], recv_sem=gather_recv.at[role, part],
            device_id=device, device_id_type=MESH,
        )

    owners = [index(*place, 0) for place in places]
    others = [index(*place, 1) for place in places]
    sent = {"all": [], "leading": [], "following": [], "helping": []}

    def send(role, part, place, device, who="all"):
        copy(role, part, owners[place], device).start()
        sent[who].append((role, part, owners[place], device))

    def arrive(role, part, place, device, dc=0):
        copy(role, part, (others if dc else owners)[place], device).wait_recv()

    def to_core(place, part, who="all"):
        send(8 + place, part, place, core_pair, who)

    def add_keyval(place):
        for dc in range(2):
            if dc == 1:
                for part in from_0:
                    arrive(8 + place, part, place, core_pair, 1)
            owner = (others if dc else owners)[place]
            cols = pl.ds(pl.multiple_of(owner * shard, shard), shard)
            kv_acc[...] += lax.dot_general(
                acts[:, cols], wt[owner], NT, preferred_element_type=jnp.float32
            )

    def add_part(place, part, dc):
        if dc == 1:
            arrive(8 + place, part, place, core_pair, 1)
        owner = (others if dc else owners)[place]
        cols = pl.ds(pl.multiple_of(owner * shard, shard), shard)
        rows = slice(parts[part][0], sum(parts[part]))
        kv_acc[:, rows] += lax.dot_general(
            acts[:, cols], wt[owner, rows, :], NT, preferred_element_type=jnp.float32
        )

    for load in loads[2:]:
        load.start()

    @pl.when(section == sections - 1)
    def _():
        load_top.start()

    @pl.when(leading)
    def _():
        for part in from_0:
            send(16, part, 0, across, "leading")

    @pl.when(helping)
    def _():
        for part in from_0:
            arrive(16, part, 0, across)
            send(17, part, 4, facing, "helping")

    for i in range(3):
        send(0, from_2[i], 0, z_next)
        send(1, from_0[i], 0, z_prev)
        send(2, from_1[i], 0, x_pair)
    for part in from_0:
        to_core(0, part)
    kv_acc[...] = jnp.zeros_like(kv_acc)
    acc[...] = jnp.zeros_like(acc)
    for i in range(3):
        arrive(0, from_2[i], 1, z_prev)

        @pl.when(jnp.logical_not(leading))
        def _():
            send(3, from_2[i], 1, z_next, "following")
            if i > 0:
                send(4, from_0[i - 1], 1, x_pair, "following")

        arrive(2, from_1[i], 3, x_pair)

        @pl.when(leading)
        def _():
            send(3, from_1[i], 3, z_next, "leading")

        send(5, from_1[i], 3, z_prev)
        arrive(1, from_0[i], 2, z_next)
        to_core(1, from_2[i])
        to_core(3, from_1[i])
        to_core(2, from_0[i])

    @pl.when(jnp.logical_not(leading))
    def _():
        send(4, from_0[2], 1, x_pair, "following")

    def relayed(part):
        @pl.when(leading)
        def _():
            arrive(17, part, 4, facing)
            send(4, part, 4, x_pair, "leading")
            to_core(4, part, "leading")

    relayed(0)
    for load in loads[2:]:
        load.wait()
    add_keyval(0)
    add_keyval(1)
    relayed(1)
    add_keyval(3)
    add_keyval(2)
    relayed(2)

    @pl.when(jnp.logical_not(leading))
    def _():
        for i in range(3):
            arrive(4, from_0[i], 6, x_pair)
            if i == 0:
                send(6, 0, 6, z_next, "following")
            arrive(5, from_1[i], 5, z_next)
            if i == 0:
                send(6, 1, 5, z_prev, "following")
            arrive(3, from_2[i], 4, z_prev)
            if i == 0:
                send(6, 2, 4, x_pair, "following")
            to_core(6, from_0[i], "following")
            to_core(5, from_1[i], "following")
            to_core(4, from_2[i], "following")
        for place in (4, 6, 5):
            add_keyval(place)
        for part, device in zip(from_0, (z_prev, z_next, x_pair)):
            arrive(6, part, 7, device)
            to_core(7, part, "following")
        add_keyval(7)

    @pl.when(leading)
    def _():
        add_keyval(4)
        for i in range(3):
            landed = ((6, from_1[i], 3, z_prev), (5, from_1[i], 5, z_next), (7, from_0[i], 4, x_pair))
            for place, part, role, device in landed:
                arrive(role, part, place, device)
                to_core(place, part, "leading")
            for dc in range(2):
                for place, part, _, _ in landed:
                    add_part(place, part, dc)

    kv[...] = kv_acc[...].astype(jnp.bfloat16)

    def place_of(chunk):
        micro = chunk // per_micro
        first = tokens - ROWS - ROWS * (chunk % per_micro)
        base = micro * tokens
        row = pl.multiple_of(base + first, ROWS)
        low = jnp.maximum(first - LONGEST, 0)
        return micro, first, row, low, pl.multiple_of(base + low, ROWS)

    def stacked(ref, row, k):
        return jnp.concatenate(
            [
                ref[pl.ds(row, ROWS), (GROUP * k + g) * HEAD_DIM:(GROUP * k + g + 1) * HEAD_DIM]
                for g in range(GROUP)
            ],
            axis=0,
        )

    def scores(chunk):
        micro, first, row, low, low_row = place_of(chunk)
        end0 = lens[micro, 0, 0]
        end1 = end0 + lens[micro, 0, 1]
        end2 = end1 + lens[micro, 0, 2]
        shape = (WINDOW, GROUP * ROWS)
        i = first + lax.broadcasted_iota(jnp.int32, (1, shape[1]), 1) % ROWS
        begin = jnp.where(i >= end2, end2, jnp.where(i >= end1, end1, jnp.where(i >= end0, end0, 0)))
        j = low + lax.broadcasted_iota(jnp.int32, shape, 0)
        allowed = (j >= begin) & (j <= i)
        for k in range(KV_HEADS):
            keys = kv[pl.ds(low_row, WINDOW), k * HEAD_DIM:(k + 1) * HEAD_DIM]
            s = lax.dot_general(keys, stacked(q, row, k), NT, preferred_element_type=jnp.float32)
            s = jnp.where(allowed, s * (math.log2(math.e) / HEAD_DIM**0.5), -1e30)
            weights = jnp.exp2(s - jnp.max(s, axis=0, keepdims=True))
            probs = weights / jnp.sum(weights, axis=0, keepdims=True)
            pt[k] = probs

    def hop(chunk, row, k):
        block = pl.ds(row, ROWS), pl.ds(k * piece, piece)
        return pltpu.make_async_remote_copy(
            src_ref=down.at[block], dst_ref=up.at[block],
            send_sem=chain_send.at[chunk, k], recv_sem=chain_recv.at[chunk, k],
            device_id=onward, device_id_type=MESH,
        )

    def step(chunk, carry):
        micro, first, row, low, low_row = place_of(chunk)
        def attend(k):
            heads = slice(k * HEAD_DIM, (k + 1) * HEAD_DIM)
            dv_heads = slice(width + k * HEAD_DIM, width + (k + 1) * HEAD_DIM)
            u = stacked(up, row, k)
            values = kv[pl.ds(low_row, WINDOW), dv_heads]
            dprobs = lax.dot_general(values, u, NT, preferred_element_type=jnp.float32)
            probs = pt[k]
            probs_rounded = probs.astype(jnp.bfloat16)
            delta = jnp.sum(probs * dprobs, axis=0, keepdims=True)
            dscores = (probs * (dprobs - delta)).astype(jnp.bfloat16)
            acc[pl.ds(low_row, WINDOW), heads] += jnp.dot(
                dscores, stacked(q, row, k), preferred_element_type=jnp.float32
            )
            acc[pl.ds(low_row, WINDOW), dv_heads] += jnp.dot(
                probs_rounded, u, preferred_element_type=jnp.float32
            )

        @pl.when(section == sections - 1)
        def _():
            for k in range(KV_HEADS):
                attend(k)
            pl.semaphore_signal(turn, inc=1, device_id=core_pair, device_id_type=MESH)
            pl.semaphore_wait(turn, 1)
            dkeys = acc[pl.ds(row, ROWS), :width] * (1.0 / HEAD_DIM**0.5)
            dkv = jnp.concatenate([dkeys, acc[pl.ds(row, ROWS), width:]], axis=1).astype(jnp.bfloat16)
            for k in range(KV_HEADS):
                for owner in range(k * piece // shard, (k + 1) * piece // shard):
                    cols = slice(owner * shard, (owner + 1) * shard)
                    back = jnp.dot(dkv, wt[owner], preferred_element_type=jnp.float32)
                    down[pl.ds(row, ROWS), cols] = (
                        up[pl.ds(row, ROWS), cols].astype(jnp.float32) + back
                    ).astype(jnp.bfloat16)
                hop(chunk, row, k).start()

        @pl.when(section < sections - 1)
        def _():
            for k in range(KV_HEADS):
                if k == 0:
                    pl.semaphore_signal(turn, inc=1, device_id=core_pair, device_id_type=MESH)
                hop(chunk, row, k).wait_recv()
                attend(k)
                if k == 3:
                    pl.semaphore_wait(turn, 1)
                heads = slice(k * HEAD_DIM, (k + 1) * HEAD_DIM)
                dv_heads = slice(width + k * HEAD_DIM, width + (k + 1) * HEAD_DIM)
                dkeys = acc[pl.ds(row, ROWS), heads] * (1.0 / HEAD_DIM**0.5)
                dkv = jnp.concatenate([dkeys, acc[pl.ds(row, ROWS), dv_heads]], axis=1).astype(jnp.bfloat16)
                for owner in range(wt.shape[0]):
                    cols = slice(owner * shard, (owner + 1) * shard)
                    weights = jnp.concatenate([wt[owner, heads, :], wt[owner, dv_heads, :]], axis=0)
                    back = jnp.dot(dkv, weights, preferred_element_type=jnp.float32)
                    if owner * shard // piece == k:
                        back += up[pl.ds(row, ROWS), cols].astype(jnp.float32)
                    if k > 0:
                        back += total[:, cols]
                    if k < KV_HEADS - 1:
                        total[:, cols] = back
                    else:
                        down[pl.ds(row, ROWS), cols] = back.astype(jnp.bfloat16)
                    done, rest = divmod((owner + 1) * shard, piece)
                    if k == KV_HEADS - 1 and rest == 0:

                        @pl.when(section > 0)
                        def _():
                            hop(chunk, row, done - 1).start()

        @pl.when(chunk < chunks - 1)
        def _():
            scores(chunk + 1)

        return carry

    scores(0)

    @pl.when(section == sections - 1)
    def _():
        load_top.wait()

    lax.fori_loop(0, chunks, step, 0)

    def finish(chunk, carry):
        row = place_of(chunk)[2]
        @pl.when(section > 0)
        def _():
            for k in range(KV_HEADS):
                hop(chunk, row, k).wait_send()

        return carry

    lax.fori_loop(0, chunks, finish, 0)
    def all_sent(who):
        for item in sent[who]:
            copy(*item).wait_send()

    all_sent("all")
    pl.when(leading)(lambda: all_sent("leading"))
    pl.when(jnp.logical_not(leading))(lambda: all_sent("following"))
    pl.when(helping)(lambda: all_sent("helping"))


def place_micros(order, grads, out, sem):
    _, micros, tokens, _ = out.shape

    def copies():
        rows = tokens // sem.shape[1]
        for k in range(micros):
            for i in range(sem.shape[1]):
                row = pl.multiple_of(order[k] * tokens + i * rows, rows)
                yield pltpu.make_async_copy(
                    grads.at[pl.ds(row, rows)], out.at[0, k, pl.ds(i * rows, rows)], sem.at[k, i]
                )

    for copy in copies():
        copy.start()
    for copy in copies():
        copy.wait()


def shards(inputs, queries, top_cotangent, key_weight, value_weight, order, doc_lengths):
    sections, fsdp = lax.axis_size("section"), lax.axis_size("fsdp")
    _, micros, tokens, features = inputs.shape
    shard, width = key_weight.shape[1:]
    rows = micros * tokens
    chunks = rows // ROWS
    bf16, f32 = jnp.bfloat16, jnp.float32
    hbm, vmem = pl.BlockSpec(memory_space=pl.ANY), pl.BlockSpec(memory_space=pltpu.VMEM)
    grads = pl.pallas_call(
        functools.partial(kernel, sections, micros, tokens),
        out_shape=pltpu.VMEM((rows, features), bf16),
        in_specs=[hbm] * 5 + [pl.BlockSpec(memory_space=pltpu.SMEM)],
        out_specs=vmem,
        scratch_shapes=[
            pltpu.VMEM((fsdp, 2 * width, shard), bf16),
            pltpu.VMEM((2 * width, shard), bf16),
            pltpu.VMEM((rows, features), bf16),
            pltpu.VMEM((rows, features), bf16),
            pltpu.VMEM((rows, features), bf16),
            pltpu.VMEM((2, shard, width), bf16),
            pltpu.VMEM((rows, 2 * width), f32),
            pltpu.VMEM((rows, 2 * width), bf16),
            pltpu.VMEM((KV_HEADS, WINDOW, GROUP * ROWS), f32),
            pltpu.VMEM((rows, 2 * width), f32),
            pltpu.VMEM((ROWS, features), f32),
            pltpu.SemaphoreType.DMA((5,)),
            pltpu.SemaphoreType.DMA((18, 3)),
            pltpu.SemaphoreType.DMA((18, 3)),
            pltpu.SemaphoreType.DMA((chunks, KV_HEADS)),
            pltpu.SemaphoreType.DMA((chunks, KV_HEADS)),
            pltpu.SemaphoreType.REGULAR,
        ],
        compiler_params=pltpu.CompilerParams(
            collective_id=0, has_side_effects=True, vmem_limit_bytes=56 << 20
        ),
        name="chain",
    )(
        inputs.reshape(rows, features),
        queries.reshape(rows, features),
        top_cotangent.reshape(rows, features),
        key_weight[0],
        value_weight[0],
        doc_lengths,
    )
    return pl.pallas_call(
        place_micros,
        out_shape=jax.ShapeDtypeStruct((1, micros, tokens, features), bf16),
        in_specs=[pl.BlockSpec(memory_space=pltpu.SMEM), vmem],
        out_specs=hbm,
        scratch_shapes=[pltpu.SemaphoreType.DMA((micros, 2))],
        compiler_params=pltpu.CompilerParams(vmem_limit_bytes=4 << 20),
        name="order",
    )(order, grads)


def solution(mesh):
    placed = (
        P("section", None, "fsdp", None),
        P("section", None, "fsdp", None),
        P(None, "fsdp", None),
        P("section", "fsdp", None),
        P("section", "fsdp", None),
        P(),
        P(None, "fsdp", None),
    )
    return jax.shard_map(
        shards,
        mesh=mesh,
        in_specs=placed,
        out_specs=P("section", None, "fsdp", None),
        check_vma=False,
    )
```

```python
import functools
import math

import jax
import jax.numpy as jnp
from jax import lax
from jax.experimental import pallas as pl
from jax.experimental.pallas import tpu as pltpu
from jax.sharding import PartitionSpec as P

MESH = pl.DeviceIdType.MESH
HEADS = 64
KV_HEADS = 4
GROUP = HEADS // KV_HEADS
HEAD_DIM = 128
ROWS = 16
LONGEST = 64
WINDOW = LONGEST + ROWS
NT = (((1,), (1,)), ((), ()))


def kernel(
    sections, micros, tokens,
    acts_hbm, q_hbm, top_hbm, kw_hbm, vw_hbm, lens, down,
    wt, relay, acts, q, up, raw, kv_acc, kv, pt, acc, total,
    load_sem, gather_send, gather_recv, chain_send, chain_recv, turn,
):
    section, f = lax.axis_index("section"), lax.axis_index("fsdp")
    z, h, c = f // 4, (f // 2) % 2, f % 2
    shard = raw.shape[1]
    width = raw.shape[2]
    piece = GROUP * HEAD_DIM
    per_micro = tokens // ROWS
    chunks = micros * per_micro

    def index(dz, dh, dc):
        return 4 * ((z + dz + 4) % 4) + 2 * ((h + dh) % 2) + (c + dc) % 2

    z_next, z_prev = (section, index(1, 0, 0)), (section, index(-1, 0, 0))
    x_pair, core_pair = (section, index(0, 1, 0)), (section, index(0, 0, 1))
    onward = ((section + sections - 1) % sections, f)
    before = ((section + 1) % sections, f)

    loads = [
        pltpu.make_async_copy(kw_hbm, raw.at[0], load_sem.at[0]),
        pltpu.make_async_copy(vw_hbm, raw.at[1], load_sem.at[1]),
        pltpu.make_async_copy(acts_hbm, acts, load_sem.at[2]),
        pltpu.make_async_copy(q_hbm, q, load_sem.at[3]),
    ]
    load_top = pltpu.make_async_copy(top_hbm, up, load_sem.at[4])
    for load in loads[:2]:
        load.start()

    leading, helping = section >= sections - 2, section < 2
    opposite = (section + 2 * jnp.where(helping, sections // 2 - 1, 1)) % sections
    facing, across = (opposite, f), (opposite, index(2, 0, 0))
    barrier = pltpu.get_barrier_semaphore()
    for device in (z_next, z_prev, x_pair, core_pair, onward, before):
        pl.semaphore_signal(barrier, inc=1, device_id=device, device_id_type=MESH)

    @pl.when(leading | helping)
    def _():
        for device in (facing, across):
            pl.semaphore_signal(barrier, inc=1, device_id=device, device_id_type=MESH)

    for part in range(2):
        loads[part].wait()
        wt[f, part * width:(part + 1) * width, :] = jnp.transpose(raw[part])

    @pl.when(leading | helping)
    def _():
        pl.semaphore_wait(barrier, 8)

    @pl.when(jnp.logical_not(leading | helping))
    def _():
        pl.semaphore_wait(barrier, 6)

    places = [(0, 0), (-1, 0), (1, 0), (0, 1), (2, 0), (1, 1), (-1, 1), (2, 1)]
    third = 3 * width // 4
    parts = [(0, 2 * width - 2 * third), (2 * width - 2 * third, third), (2 * width - third, third)]
    from_0, from_1, from_2 = (0, 1, 2), (1, 2, 0), (2, 0, 1)

    def copy(role, part, owner, device):
        first, size = parts[part]
        rows = pl.ds(first, size)
        source = relay.at[rows, :] if role == 17 else wt.at[owner, rows, :]
        target = relay.at[rows, :] if role == 16 else wt.at[owner, rows, :]
        return pltpu.make_async_remote_copy(
            src_ref=source, dst_ref=target,
            send_sem=gather_send.at[role, part], recv_sem=gather_recv.at[role, part],
            device_id=device, device_id_type=MESH,
        )

    owners = [index(*place, 0) for place in places]
    others = [index(*place, 1) for place in places]
    sent = {"all": [], "leading": [], "following": [], "helping": []}

    def send(role, part, place, device, who="all"):
        copy(role, part, owners[place], device).start()
        sent[who].append((role, part, owners[place], device))

    def arrive(role, part, place, device, dc=0):
        copy(role, part, (others if dc else owners)[place], device).wait_recv()

    def to_core(place, part, who="all"):
        send(8 + place, part, place, core_pair, who)

    def add_keyval(place):
        for dc in range(2):
            if dc == 1:
                for part in from_0:
                    arrive(8 + place, part, place, core_pair, 1)
            owner = (others if dc else owners)[place]
            cols = pl.ds(pl.multiple_of(owner * shard, shard), shard)
            kv_acc[...] += lax.dot_general(
                acts[:, cols], wt[owner], NT, preferred_element_type=jnp.float32
            )

    def add_part(place, part, dc):
        if dc == 1:
            arrive(8 + place, part, place, core_pair, 1)
        owner = (others if dc else owners)[place]
        cols = pl.ds(pl.multiple_of(owner * shard, shard), shard)
        rows = slice(parts[part][0], sum(parts[part]))
        kv_acc[:, rows] += lax.dot_general(
            acts[:, cols], wt[owner, rows, :], NT, preferred_element_type=jnp.float32
        )

    for load in loads[2:]:
        load.start()

    @pl.when(section == sections - 1)
    def _():
        load_top.start()

    @pl.when(leading)
    def _():
        for part in from_0:
            send(16, part, 0, across, "leading")

    @pl.when(helping)
    def _():
        for part in from_0:
            arrive(16, part, 0, across)
            send(17, part, 4, facing, "helping")

    for i in range(3):
        send(0, from_2[i], 0, z_next)
        send(1, from_0[i], 0, z_prev)
        send(2, from_1[i], 0, x_pair)
    for part in from_0:
        to_core(0, part)
    kv_acc[...] = jnp.zeros_like(kv_acc)
    acc[...] = jnp.zeros_like(acc)
    for i in range(3):
        arrive(0, from_2[i], 1, z_prev)

        @pl.when(jnp.logical_not(leading))
        def _():
            send(3, from_2[i], 1, z_next, "following")
            if i > 0:
                send(4, from_0[i - 1], 1, x_pair, "following")

        arrive(2, from_1[i], 3, x_pair)

        @pl.when(leading)
        def _():
            send(3, from_1[i], 3, z_next, "leading")

        send(5, from_1[i], 3, z_prev)
        arrive(1, from_0[i], 2, z_next)
        to_core(1, from_2[i])
        to_core(3, from_1[i])
        to_core(2, from_0[i])

    @pl.when(jnp.logical_not(leading))
    def _():
        send(4, from_0[2], 1, x_pair, "following")

    def relayed(part):
        @pl.when(leading)
        def _():
            arrive(17, part, 4, facing)
            send(4, part, 4, x_pair, "leading")
            to_core(4, part, "leading")

    relayed(0)
    for load in loads[2:]:
        load.wait()
    add_keyval(0)
    add_keyval(1)
    relayed(1)
    add_keyval(3)
    add_keyval(2)
    relayed(2)

    @pl.when(jnp.logical_not(leading))
    def _():
        for i in range(3):
            arrive(4, from_0[i], 6, x_pair)
            if i == 0:
                send(6, 0, 6, z_next, "following")
            arrive(5, from_1[i], 5, z_next)
            if i == 0:
                send(6, 1, 5, z_prev, "following")
            arrive(3, from_2[i], 4, z_prev)
            if i == 0:
                send(6, 2, 4, x_pair, "following")
            to_core(6, from_0[i], "following")
            to_core(5, from_1[i], "following")
            to_core(4, from_2[i], "following")
        for place in (4, 6, 5):
            add_keyval(place)
        for part, device in zip(from_0, (z_prev, z_next, x_pair)):
            arrive(6, part, 7, device)
            to_core(7, part, "following")
        add_keyval(7)

    @pl.when(leading)
    def _():
        add_keyval(4)
        for i in range(3):
            landed = ((6, from_1[i], 3, z_prev), (5, from_1[i], 5, z_next), (7, from_0[i], 4, x_pair))
            for place, part, role, device in landed:
                arrive(role, part, place, device)
                to_core(place, part, "leading")
            for dc in range(2):
                for place, part, _, _ in landed:
                    add_part(place, part, dc)

    kv[...] = kv_acc[...].astype(jnp.bfloat16)

    def place_of(chunk):
        micro = chunk // per_micro
        first = tokens - ROWS - ROWS * (chunk % per_micro)
        base = micro * tokens
        row = pl.multiple_of(base + first, ROWS)
        low = jnp.maximum(first - LONGEST, 0)
        return micro, first, row, low, pl.multiple_of(base + low, ROWS)

    def stacked(ref, row, k):
        return jnp.concatenate(
            [
                ref[pl.ds(row, ROWS), (GROUP * k + g) * HEAD_DIM:(GROUP * k + g + 1) * HEAD_DIM]
                for g in range(GROUP)
            ],
            axis=0,
        )

    def scores(chunk):
        micro, first, row, low, low_row = place_of(chunk)
        end0 = lens[micro, 0, 0]
        end1 = end0 + lens[micro, 0, 1]
        end2 = end1 + lens[micro, 0, 2]
        shape = (WINDOW, GROUP * ROWS)
        i = first + lax.broadcasted_iota(jnp.int32, (1, shape[1]), 1) % ROWS
        begin = jnp.where(i >= end2, end2, jnp.where(i >= end1, end1, jnp.where(i >= end0, end0, 0)))
        j = low + lax.broadcasted_iota(jnp.int32, shape, 0)
        allowed = (j >= begin) & (j <= i)
        for k in range(KV_HEADS):
            keys = kv[pl.ds(low_row, WINDOW), k * HEAD_DIM:(k + 1) * HEAD_DIM]
            s = lax.dot_general(keys, stacked(q, row, k), NT, preferred_element_type=jnp.float32)
            s = jnp.where(allowed, s * (math.log2(math.e) / HEAD_DIM**0.5), -1e30)
            weights = jnp.exp2(s - jnp.max(s, axis=0, keepdims=True))
            probs = weights / jnp.sum(weights, axis=0, keepdims=True)
            pt[k] = probs

    def hop(chunk, row, k):
        block = pl.ds(row, ROWS), pl.ds(k * piece, piece)
        return pltpu.make_async_remote_copy(
            src_ref=down.at[block], dst_ref=up.at[block],
            send_sem=chain_send.at[chunk, k], recv_sem=chain_recv.at[chunk, k],
            device_id=onward, device_id_type=MESH,
        )

    def step(chunk, carry):
        micro, first, row, low, low_row = place_of(chunk)
        def attend(k):
            heads = slice(k * HEAD_DIM, (k + 1) * HEAD_DIM)
            dv_heads = slice(width + k * HEAD_DIM, width + (k + 1) * HEAD_DIM)
            u = stacked(up, row, k)
            values = kv[pl.ds(low_row, WINDOW), dv_heads]
            dprobs = lax.dot_general(values, u, NT, preferred_element_type=jnp.float32)
            probs = pt[k]
            probs_rounded = probs.astype(jnp.bfloat16)
            delta = jnp.sum(probs * dprobs, axis=0, keepdims=True)
            dscores = (probs * (dprobs - delta)).astype(jnp.bfloat16)
            acc[pl.ds(low_row, WINDOW), heads] += jnp.dot(
                dscores, stacked(q, row, k), preferred_element_type=jnp.float32
            )
            acc[pl.ds(low_row, WINDOW), dv_heads] += jnp.dot(
                probs_rounded, u, preferred_element_type=jnp.float32
            )

        @pl.when(section == sections - 1)
        def _():
            for k in range(KV_HEADS):
                attend(k)
            pl.semaphore_signal(turn, inc=1, device_id=core_pair, device_id_type=MESH)
            pl.semaphore_wait(turn, 1)
            dkeys = acc[pl.ds(row, ROWS), :width] * (1.0 / HEAD_DIM**0.5)
            dkv = jnp.concatenate([dkeys, acc[pl.ds(row, ROWS), width:]], axis=1).astype(jnp.bfloat16)
            for k in range(KV_HEADS):
                for owner in range(k * piece // shard, (k + 1) * piece // shard):
                    cols = slice(owner * shard, (owner + 1) * shard)
                    back = jnp.dot(dkv, wt[owner], preferred_element_type=jnp.float32)
                    down[pl.ds(row, ROWS), cols] = (
                        up[pl.ds(row, ROWS), cols].astype(jnp.float32) + back
                    ).astype(jnp.bfloat16)
                hop(chunk, row, k).start()

        @pl.when(section < sections - 1)
        def _():
            for k in range(KV_HEADS):
                if k == 0:
                    pl.semaphore_signal(turn, inc=1, device_id=core_pair, device_id_type=MESH)
                if k == KV_HEADS - 1:
                    pl.semaphore_wait(turn, 1)
                hop(chunk, row, k).wait_recv()
                attend(k)
                heads = slice(k * HEAD_DIM, (k + 1) * HEAD_DIM)
                dv_heads = slice(width + k * HEAD_DIM, width + (k + 1) * HEAD_DIM)
                dkeys = acc[pl.ds(row, ROWS), heads] * (1.0 / HEAD_DIM**0.5)
                dkv = jnp.concatenate([dkeys, acc[pl.ds(row, ROWS), dv_heads]], axis=1).astype(jnp.bfloat16)
                for owner in range(wt.shape[0]):
                    cols = slice(owner * shard, (owner + 1) * shard)
                    weights = jnp.concatenate([wt[owner, heads, :], wt[owner, dv_heads, :]], axis=0)
                    back = jnp.dot(dkv, weights, preferred_element_type=jnp.float32)
                    if owner * shard // piece == k:
                        back += up[pl.ds(row, ROWS), cols].astype(jnp.float32)
                    if k > 0:
                        back += total[:, cols]
                    if k < KV_HEADS - 1:
                        total[:, cols] = back
                    else:
                        down[pl.ds(row, ROWS), cols] = back.astype(jnp.bfloat16)
                    done, rest = divmod((owner + 1) * shard, piece)
                    if k == KV_HEADS - 1 and rest == 0:

                        @pl.when(section > 0)
                        def _():
                            hop(chunk, row, done - 1).start()

        @pl.when(chunk < chunks - 1)
        def _():
            scores(chunk + 1)

        return carry

    scores(0)

    @pl.when(section == sections - 1)
    def _():
        load_top.wait()

    lax.fori_loop(0, chunks, step, 0)

    def finish(chunk, carry):
        row = place_of(chunk)[2]
        @pl.when(section > 0)
        def _():
            for k in range(KV_HEADS):
                hop(chunk, row, k).wait_send()

        return carry

    lax.fori_loop(0, chunks, finish, 0)
    def all_sent(who):
        for item in sent[who]:
            copy(*item).wait_send()

    all_sent("all")
    pl.when(leading)(lambda: all_sent("leading"))
    pl.when(jnp.logical_not(leading))(lambda: all_sent("following"))
    pl.when(helping)(lambda: all_sent("helping"))


def place_micros(order, grads, out, sem):
    _, micros, tokens, _ = out.shape

    def copies():
        rows = tokens // sem.shape[1]
        for k in range(micros):
            for i in range(sem.shape[1]):
                row = pl.multiple_of(order[k] * tokens + i * rows, rows)
                yield pltpu.make_async_copy(
                    grads.at[pl.ds(row, rows)], out.at[0, k, pl.ds(i * rows, rows)], sem.at[k, i]
                )

    for copy in copies():
        copy.start()
    for copy in copies():
        copy.wait()


def shards(inputs, queries, top_cotangent, key_weight, value_weight, order, doc_lengths):
    sections, fsdp = lax.axis_size("section"), lax.axis_size("fsdp")
    _, micros, tokens, features = inputs.shape
    shard, width = key_weight.shape[1:]
    rows = micros * tokens
    chunks = rows // ROWS
    bf16, f32 = jnp.bfloat16, jnp.float32
    hbm, vmem = pl.BlockSpec(memory_space=pl.ANY), pl.BlockSpec(memory_space=pltpu.VMEM)
    grads = pl.pallas_call(
        functools.partial(kernel, sections, micros, tokens),
        out_shape=pltpu.VMEM((rows, features), bf16),
        in_specs=[hbm] * 5 + [pl.BlockSpec(memory_space=pltpu.SMEM)],
        out_specs=vmem,
        scratch_shapes=[
            pltpu.VMEM((fsdp, 2 * width, shard), bf16),
            pltpu.VMEM((2 * width, shard), bf16),
            pltpu.VMEM((rows, features), bf16),
            pltpu.VMEM((rows, features), bf16),
            pltpu.VMEM((rows, features), bf16),
            pltpu.VMEM((2, shard, width), bf16),
            pltpu.VMEM((rows, 2 * width), f32),
            pltpu.VMEM((rows, 2 * width), bf16),
            pltpu.VMEM((KV_HEADS, WINDOW, GROUP * ROWS), f32),
            pltpu.VMEM((rows, 2 * width), f32),
            pltpu.VMEM((ROWS, features), f32),
            pltpu.SemaphoreType.DMA((5,)),
            pltpu.SemaphoreType.DMA((18, 3)),
            pltpu.SemaphoreType.DMA((18, 3)),
            pltpu.SemaphoreType.DMA((chunks, KV_HEADS)),
            pltpu.SemaphoreType.DMA((chunks, KV_HEADS)),
            pltpu.SemaphoreType.REGULAR,
        ],
        compiler_params=pltpu.CompilerParams(
            collective_id=0, has_side_effects=True, vmem_limit_bytes=56 << 20
        ),
        name="chain",
    )(
        inputs.reshape(rows, features),
        queries.reshape(rows, features),
        top_cotangent.reshape(rows, features),
        key_weight[0],
        value_weight[0],
        doc_lengths,
    )
    return pl.pallas_call(
        place_micros,
        out_shape=jax.ShapeDtypeStruct((1, micros, tokens, features), bf16),
        in_specs=[pl.BlockSpec(memory_space=pltpu.SMEM), vmem],
        out_specs=hbm,
        scratch_shapes=[pltpu.SemaphoreType.DMA((micros, 2))],
        compiler_params=pltpu.CompilerParams(vmem_limit_bytes=4 << 20),
        name="order",
    )(order, grads)


def solution(mesh):
    placed = (
        P("section", None, "fsdp", None),
        P("section", None, "fsdp", None),
        P(None, "fsdp", None),
        P("section", "fsdp", None),
        P("section", "fsdp", None),
        P(),
        P(None, "fsdp", None),
    )
    return jax.shard_map(
        shards,
        mesh=mesh,
        in_specs=placed,
        out_specs=P("section", None, "fsdp", None),
        check_vma=False,
    )
```
